32 devices in a mesh: group: 2 (over x), replica: 16 (over z, y, core).
Axes of the slice: x: 2, y: 2, z: 4, core: 2. Of those that a mesh axis runs over, the one named last changes fastest.
Arguments:
- images: bfloat16 [2, 16, 4, 14, 14, 256], P(None, 'replica', 'group'), may hold values from -6 to 6
- labels: int32 [2, 16, 4], P(None, 'replica', 'group'), may hold values from 0 to 999
- step_index: int32 [1], replicated, may hold values from 0 to 63
- weights: float32 [16, 3, 3, 256, 256], P('replica', None, None, 'group'), may hold values from -4 to 4
- velocity: float32 [16, 3, 3, 256, 256], P('replica', None, None, 'group'), may hold values from -3 to 3
- head_weight: bfloat16 [1000, 256], replicated, may hold values from -3 to 3
Outputs:
- new_weights: float32 [16, 3, 3, 256, 256], P('replica', None, None, 'group')
- new_velocity: float32 [16, 3, 3, 256, 256], P('replica', None, None, 'group')
- input_grads: bfloat16 [2, 16, 4, 14, 14, 256], P(None, 'replica', 'group')
The draws below stay inside these ranges and needn't reach their ends.
All inputs are finite; a program needn't handle non-finite values.
Results may differ from the reference program's by a relative error of at most 0.035.
Values may be sent and summed in bfloat16 or wider, within the bound.
No kernel may reach another device: no remote copies, remote signals or barrier semaphores. Data moves between devices by JAX's collectives and lax.ppermute only.
A program may use at most 64 MiB of HBM per device.

```python
import math
import jax
import jax.numpy as jnp
from jax import lax

C = 256
CLASSES = 1000
HW = 14
KS = 3
ITERS = 2
IMG_DEV = 2
IMAGES = 4
N_GROUP = 2
N_REPLICA = 16


def place_ends(array, key, smallest, high):
    longest = array.shape.index(max(array.shape))
    spots = []
    for shift in (0, 1):
        where = [jax.random.randint(jax.random.fold_in(key, axis), (), 0, length) for axis, length in enumerate(array.shape)]
        where[longest] = (where[longest] + shift) % array.shape[longest]
        spots.append(tuple(where))
    return array.at[spots[0]].set(smallest).at[spots[1]].set(high)


def steps_of(key, shape, pieces, least, high):
    gain, own = 1.0, jax.random.fold_in(key, 6)
    for position, blocks in pieces:
        draws = jnp.exp(jax.random.uniform(jax.random.fold_in(own, position), (blocks,), jnp.float32, least / len(pieces), high / len(pieces)))
        gain = gain * jnp.repeat(draws, shape[position] // blocks).reshape([-1 if axis == position else 1 for axis in range(len(shape))])
    return gain


def noise(key, dims, width, most, split=(), held_as=jnp.bfloat16):
    entries = jax.random.normal(key, dims, jnp.float32) * width
    if len(split) > 0:
        entries = steps_of(key, dims, split, -0.22, 0.18) * entries
    return jnp.clip(entries, min=-most, max=most).astype(held_as)


def setup_inputs(seed: int = 0) -> dict:
    streams_of = jax.random.split(jax.random.key(seed), 7)
    return {
        "images": noise(streams_of[0], (ITERS, N_REPLICA, IMAGES, HW, HW, C), 1.0, 6.0, ((1, 16), (2, 2))),
        "labels": place_ends(jax.random.randint(streams_of[1], (ITERS, N_REPLICA, IMAGES), 0, CLASSES), jax.random.fold_in(streams_of[1], 1), 0, CLASSES - 1).astype(jnp.int32),
        "step_index": jax.random.randint(streams_of[2], (1,), 0, 64).astype(jnp.int32),
        "weights": noise(streams_of[3], (N_REPLICA, KS, KS, C, C), 1.0, 4.0, ((0, 16), (3, 2)), jnp.float32),
        "velocity": noise(streams_of[4], (N_REPLICA, KS, KS, C, C), 0.5, 3.0, ((0, 16), (3, 2)), jnp.float32),
        "head_weight": noise(streams_of[5], (CLASSES, C), 0.5, 3.0),
    }


MOMENTUM = 0.9
LOSS_SCALE = 256.0

def convolve(inputs, kernel):
    return lax.conv_general_dilated(inputs, kernel, (1, 1), 'SAME', dimension_numbers=('NHWC', 'HWIO', 'NHWC'), preferred_element_type=jnp.float32)

def weight_terms(inputs, grad_out):
    edge = inputs.shape[1]
    padded = jnp.pad(inputs.astype(jnp.float32), ((0, 0), (1, 1), (1, 1), (0, 0)))
    upper = grad_out.astype(jnp.float32)
    stacked = []
    for row_off in range(KS):
        line = []
        for col_off in range(KS):
            window = padded[:, row_off:row_off + edge, col_off:col_off + edge, :]
            line.append(jnp.einsum('nijq,nijo->qo', window, upper))
        stacked.append(jnp.stack(line))
    return jnp.stack(stacked)

def rounded(values):
    return lax.optimization_barrier(values.astype(jnp.bfloat16)).astype(jnp.float32)

def local_step(weights, velocity, inputs, targets, head_weight):
    conv_scale = 1.0 / math.sqrt(KS * KS * C)
    step_size = 0.1 * KS * KS * C
    kernel = weights.astype(jnp.bfloat16)
    preact = convolve(inputs, kernel) * conv_scale
    sigmoid_pre = jax.nn.sigmoid(preact)
    pooled = lax.optimization_barrier(jnp.mean(preact * sigmoid_pre, axis=(1, 2))).astype(jnp.bfloat16)
    logits = jnp.dot(pooled, head_weight.T, preferred_element_type=jnp.float32)
    expo = jnp.exp(logits - lax.optimization_barrier(jnp.max(logits, axis=1, keepdims=True)))
    probs = expo / lax.optimization_barrier(jnp.sum(expo, axis=1, keepdims=True))
    onehot = (targets[:, None] == jnp.arange(CLASSES, dtype=jnp.int32)[None, :]).astype(jnp.float32)
    dlogits = (LOSS_SCALE * (probs - onehot)).astype(jnp.bfloat16)
    dpooled = jnp.dot(dlogits, head_weight, preferred_element_type=jnp.float32)
    grad_out = (sigmoid_pre * (1.0 + preact * (1.0 - sigmoid_pre)) * dpooled[:, None, None, :] / (HW * HW)).astype(jnp.bfloat16)
    flipped = jnp.swapaxes(jnp.flip(kernel, (0, 1)), 2, 3)
    grad_in = (convolve(grad_out, flipped) * conv_scale).astype(jnp.bfloat16)
    block_in = inputs.reshape(N_GROUP, IMG_DEV, HW, HW, C)
    block_out = grad_out.reshape(N_GROUP, IMG_DEV, HW, HW, C)
    partials = jax.vmap(weight_terms)(block_in, block_out) * conv_scale
    grad = lax.optimization_barrier(jnp.sum(rounded(partials), axis=0)) / LOSS_SCALE
    new_velocity = MOMENTUM * velocity - step_size * grad
    half_weights = weights + MOMENTUM * new_velocity - step_size * grad
    return (half_weights, new_velocity, grad_in)

def reference(images, labels, step_index, weights, velocity, head_weight):
    bits = N_REPLICA.bit_length() - 1
    grads_in = []
    for turn in range(ITERS):

        def per_replica(packed):
            return local_step(packed[0], packed[1], packed[2], packed[3], head_weight)
        half_weights, velocity, grad_in = lax.map(per_replica, (weights, velocity, images[turn], labels[turn]))
        select = ((step_index[0] + turn) % bits).astype(jnp.int32)
        distance = jnp.left_shift(jnp.int32(1), select)
        weights = 0.5 * (half_weights + jnp.roll(half_weights, distance, axis=0))
        grads_in.append(grad_in)
    return (weights, velocity, jnp.stack(grads_in))
```

```python
from functools import partial
import math

import jax
import jax.numpy as jnp
from jax import lax
from jax.experimental import pallas as pl
from jax.experimental.pallas import tpu as pltpu
from jax.sharding import PartitionSpec as P

ITERS = 2

MOMENTUM = 0.9
LOSS_SCALE = 256.0
LINE = 16


def shifted(x, axis, by):
    length = lax.axis_size(axis)
    return lax.ppermute(x, axis, [(i, (i + by) % length) for i in range(length)])


def columns_beside(maps):
    n, high, wide, q = maps.shape
    padded = jnp.pad(maps, ((0, 0), (1, 1), (1, LINE + 1 - wide), (0, 0)))
    beside = jnp.concatenate([padded[:, :, b : b + LINE] for b in range(3)], axis=3)
    return beside.reshape(n, (high + 2) * LINE, 3 * q)


def conv_rows(x_ref, kernel_of, n, rows):
    total = None
    for a in range(3):
        term = jnp.dot(
            x_ref[n, a * LINE : a * LINE + rows, :], kernel_of(a), preferred_element_type=jnp.float32
        )
        total = term if total is None else total + term
    return total


def first_forward_kernel(rows, x_ref, w_ref, pre_ref, sent_ref, kernel_ref):
    depth = w_ref.shape[0] // 3
    kernel_ref[...] = w_ref[...].astype(jnp.bfloat16)
    for n in range(x_ref.shape[0]):
        part = conv_rows(x_ref, lambda a: kernel_ref[a * depth : (a + 1) * depth, :], n, rows)
        pre_ref[n] = part
        sent_ref[n] = part.astype(jnp.bfloat16)


def forward_kernel(rows, x_ref, kernel_ref, pre_ref, sent_ref):
    depth = kernel_ref.shape[0] // 3
    for n in range(x_ref.shape[0]):
        part = conv_rows(x_ref, lambda a: kernel_ref[a * depth : (a + 1) * depth, :], n, rows)
        pre_ref[n] = part
        sent_ref[n] = part.astype(jnp.bfloat16)


def merged_forward_kernel(rows, x_ref, half_ref, peer_ref, pre_ref, sent_ref, w_ref, kernel_ref):
    depth = half_ref.shape[0] // 3
    merged = 0.5 * (half_ref[...] + peer_ref[...].astype(jnp.float32))
    w_ref[...] = merged
    kernel_ref[...] = merged.astype(jnp.bfloat16)
    for n in range(x_ref.shape[0]):
        part = conv_rows(x_ref, lambda a: kernel_ref[a * depth : (a + 1) * depth, :], n, rows)
        pre_ref[n] = part
        sent_ref[n] = part.astype(jnp.bfloat16)


def backward_kernel(
    wide, classes, scale, step_size, swap, x_ref, own_ref, other_ref, labels_ref, head_ref, w_ref, v_ref,
    half_ref, sent_ref, new_v_ref, grad_ref, pre_ref, sig_ref,
):
    images, rows, chan = own_ref.shape
    area = wide * (rows // LINE)
    depth = w_ref.shape[0] // 3
    real = lax.broadcasted_iota(jnp.int32, (rows, chan), 0) % LINE < wide
    pooled = []
    for n in range(images):
        other = other_ref[(n + swap) % images].astype(jnp.float32)
        pre = (own_ref[n] + other) * scale
        sig = jax.nn.sigmoid(pre)
        pre_ref[n] = pre
        sig_ref[n] = sig
        pooled.append(jnp.sum(jnp.where(real, pre * sig, 0.0), axis=0, keepdims=True) / area)
    pooled = jnp.concatenate(pooled, axis=0).astype(jnp.bfloat16)
    logits = lax.dot_general(
        pooled, head_ref[...], (((1,), (1,)), ((), ())), preferred_element_type=jnp.float32
    )
    klass = lax.broadcasted_iota(jnp.int32, logits.shape, 1)
    logits = jnp.where(klass < classes, logits, -jnp.inf)
    expo = jnp.exp(logits - jnp.max(logits, axis=1, keepdims=True))
    probs = expo / jnp.sum(expo, axis=1, keepdims=True)
    onehot = (labels_ref[...] == klass).astype(jnp.float32)
    dlogits = (LOSS_SCALE * (probs - onehot)).astype(jnp.bfloat16)
    dpooled = jnp.dot(dlogits, head_ref[...], preferred_element_type=jnp.float32) / area
    for n in range(images):
        pre = pre_ref[n]
        sig = sig_ref[n]
        slope = sig * (1.0 + pre * (1.0 - sig)) * dpooled[n : n + 1]
        grad_ref[n] = jnp.where(real, slope, 0.0).astype(jnp.bfloat16)
    for a in range(3):
        total = None
        for n in range(images):
            term = lax.dot_general(
                x_ref[n, a * LINE : a * LINE + rows, :],
                grad_ref[n],
                (((0,), (0,)), ((), ())),
                preferred_element_type=jnp.float32,
            )
            total = term if total is None else total + term
        part = slice(a * depth, (a + 1) * depth)
        step = total * (step_size * scale / LOSS_SCALE)
        new_v = MOMENTUM * v_ref[part, :] - step
        half = w_ref[part, :] + MOMENTUM * new_v - step
        new_v_ref[part, :] = new_v
        half_ref[part, :] = half
        sent_ref[part, :] = half.astype(jnp.bfloat16)


PARAMS = pltpu.CompilerParams(vmem_limit_bytes=40 * 1024 * 1024)


def f32(*shape):
    return jax.ShapeDtypeStruct(shape, jnp.float32)


def b16(*shape):
    return jax.ShapeDtypeStruct(shape, jnp.bfloat16)


def first_forward(x, w, rows):
    n, chan = x.shape[0], w.shape[1]
    return pl.pallas_call(
        partial(first_forward_kernel, rows),
        out_shape=(f32(n, rows, chan), b16(n, rows, chan), b16(*w.shape)),
        compiler_params=PARAMS,
        name="first_forward",
    )(x, w)


def forward(x, kernel, rows):
    n, chan = x.shape[0], kernel.shape[1]
    return pl.pallas_call(
        partial(forward_kernel, rows),
        out_shape=(f32(n, rows, chan), b16(n, rows, chan)),
        compiler_params=PARAMS,
        name="forward",
    )(x, kernel)


def merged_forward(x, half, peer, rows):
    n, chan = x.shape[0], half.shape[1]
    return pl.pallas_call(
        partial(merged_forward_kernel, rows),
        out_shape=(f32(n, rows, chan), b16(n, rows, chan), f32(*half.shape), b16(*half.shape)),
        compiler_params=PARAMS,
        name="merged_forward",
    )(x, half, peer)


def backward(x, own, other, labels, head, w, v, wide, classes, swap):
    images, rows, chan = own.shape
    scale = 1.0 / math.sqrt(9 * chan)
    step_size = 0.1 * 9 * chan
    return pl.pallas_call(
        partial(backward_kernel, wide, classes, scale, step_size, swap),
        out_shape=(f32(*w.shape), b16(*w.shape), f32(*w.shape), b16(images, rows, chan)),
        scratch_shapes=[pltpu.VMEM((images, rows, chan), jnp.float32)] * 2,
        compiler_params=PARAMS,
        name="backward",
    )(x, own, other, labels, head, w, v)


def input_gradient(grad_out, kernel, wide):
    n, rows, chan = grad_out.shape
    high = rows // LINE
    maps = grad_out.reshape(n, high, LINE, chan)[:, :, :wide]
    taps = kernel.reshape(3, 3, kernel.shape[0] // 9, chan)
    flipped = jnp.swapaxes(jnp.flip(taps, (0, 1)), 2, 3)
    out = lax.conv_general_dilated(
        maps,
        flipped,
        (1, 1),
        "SAME",
        dimension_numbers=("NHWC", "HWIO", "NHWC"),
        preferred_element_type=jnp.float32,
    )
    return (out * (1.0 / math.sqrt(9 * chan))).astype(jnp.bfloat16)


def run(select, images, labels, weights, velocity, head_weight):
    images, labels = images[:, 0], labels[:, 0]
    _, mine, high, wide, chan = images.shape
    share = weights.shape[3]
    members = lax.axis_size("group")
    me = lax.axis_index("group")
    bits = lax.axis_size("replica").bit_length() - 1
    classes = head_weight.shape[0]
    rows = high * LINE
    w = weights.reshape(9 * share, chan)
    v = velocity.reshape(9 * share, chan)
    head = jnp.pad(head_weight, ((0, -classes % 128), (0, 0)))
    pair = members == 2
    if pair:
        theirs = lax.dynamic_slice_in_dim(images, (1 - me) * share, share, axis=4)
        came = shifted(theirs, "group", 1)
        all_labels = jnp.concatenate([labels, shifted(labels, "group", 1)], axis=1)
        kept = lax.dynamic_slice_in_dim(images, me * share, share, axis=4)
    else:
        maps = lax.all_to_all(images, "group", split_axis=4, concat_axis=1, tiled=True)
        all_labels = lax.all_gather(labels, "group", axis=1, tiled=True)

    def exchange(pre, sent):
        if pair:
            return shifted(sent, "group", 1)
        return lax.psum(pre, "group") - pre

    grads_in = []
    for turn in range(ITERS):
        distance = 1 << ((select + turn) % bits)
        if pair:
            x_own, x_came = columns_beside(kept[turn]), columns_beside(came[turn])
            x = jnp.concatenate([x_own, x_came])
        else:
            x = columns_beside(maps[turn])
        if turn > 0:
            own, sent, w, kernel = merged_forward(x, half, peer, rows)
            other = exchange(own, sent)
        elif pair:
            own_a, sent_a, kernel = first_forward(x_own, w, rows)
            other_b = shifted(sent_a, "group", 1)
            own_b, sent_b = forward(x_came, kernel, rows)
            other_a = shifted(sent_b, "group", 1)
            own = jnp.concatenate([own_a, own_b])
            other = jnp.concatenate([other_b, other_a])
        else:
            own, sent, kernel = first_forward(x, w, rows)
            other = exchange(own, sent)
        half, sent, v, grad_out = backward(
            x, own, other, all_labels[turn][:, None], head, w, v, wide, classes, mine if pair else 0
        )
        peer = shifted(sent, "replica", distance)
        grad_in = input_gradient(grad_out, kernel, wide)
        if pair:
            back = shifted(grad_in[mine:], "group", 1)
            low = jnp.where(me == 0, grad_in[:mine], back)
            top = jnp.where(me == 0, back, grad_in[:mine])
            grads_in.append(jnp.concatenate([low, top], axis=3))
        else:
            grads_in.append(lax.all_to_all(grad_in, "group", split_axis=0, concat_axis=3, tiled=True))
    w = 0.5 * (half + peer.astype(jnp.float32))
    shape = weights.shape
    return (w.reshape(shape), v.reshape(shape), jnp.stack(grads_in)[:, None])


def local(images, labels, step_index, weights, velocity, head_weight):
    bits = lax.axis_size("replica").bit_length() - 1
    return lax.switch(
        step_index[0] % bits,
        [partial(run, select) for select in range(bits)],
        images,
        labels,
        weights,
        velocity,
        head_weight,
    )


def solution(mesh):
    return jax.shard_map(
        local,
        mesh=mesh,
        in_specs=(
            P(None, "replica", "group", None, None, None),
            P(None, "replica", "group"),
            P(),
            P("replica", None, None, "group", None),
            P("replica", None, None, "group", None),
            P(),
        ),
        out_specs=(
            P("replica", None, None, "group", None),
            P("replica", None, None, "group", None),
            P(None, "replica", "group", None, None, None),
        ),
        check_vma=False,
    )
```

```python
from functools import partial
import math

import jax
import jax.numpy as jnp
from jax import lax
from jax.experimental import pallas as pl
from jax.experimental.pallas import tpu as pltpu
from jax.sharding import PartitionSpec as P

ITERS = 2

MOMENTUM = 0.9
LOSS_SCALE = 256.0
LINE = 16
SUB = 8


def shifted(x, axis, by):
    length = lax.axis_size(axis)
    return lax.ppermute(x, axis, [(i, (i + by) % length) for i in range(length)])


def line_by_line(dst, src, lines, wide, to, at, start=0):
    for i in range(lines):
        dst[start + i * to : start + i * to + wide, :] = src[i * at : i * at + wide, :]


def columns_beside(x_ref, flat, spread, m, high):
    wide, step = x_ref.shape[0] // high, LINE * m
    flat[...] = x_ref[...].astype(jnp.float32)
    spread[...] = jnp.zeros_like(spread)
    line_by_line(spread, flat, high, wide, step, wide, step)
    rows = spread[...]
    beside = [pltpu.roll(rows, m, 0), rows, pltpu.roll(rows, rows.shape[0] - m, 0)]
    return [part.astype(jnp.bfloat16) for part in beside]


def forward_kernel(blocks, m, high, cast, merge, *refs):
    refs = list(refs)
    x_refs, refs = refs[:blocks], refs[blocks:]
    wide, step = x_refs[0].shape[0] // high, LINE * m
    rows = high * step
    if cast:
        w_hbm, *pre_refs, sent_ref, kernel_ref, kernel_hbm, flat, spread, w, kernel, sems, out_sem = refs
    elif merge:
        w_hbm, peer_hbm, *pre_refs, sent_ref, kernel_hbm, flat, spread, w, kernel, sems, out_sem, peer, peer_sems = refs
    else:
        kernel_ref, *pre_refs, sent_ref, flat, spread = refs
    copies = []
    if cast or merge:
        depth = w.shape[0] // 3
        parts = [pl.ds(a * depth, depth) for a in range(3)]
        copies = [[pltpu.make_async_copy(w_hbm.at[p], w.at[p], sems.at[a])] for a, p in enumerate(parts)]
        if merge:
            for a, p in enumerate(parts):
                copies[a].append(pltpu.make_async_copy(peer_hbm.at[p], peer.at[p], peer_sems.at[a]))
        for part in copies:
            for copy in part:
                copy.start()
    taps = []
    for n in range(blocks):
        beside = columns_beside(x_refs[n], flat, spread, m, high)
        lines = [part[a * step : a * step + rows] for a in range(3) for part in beside]
        taps.append(jnp.concatenate(lines, axis=1))
    if cast or merge:
        for a, p in enumerate(parts):
            for copy in copies[a]:
                copy.wait()
            part = w[p, :]
            if merge:
                part = 0.5 * (part + peer[p, :].astype(jnp.float32))
            kernel[p, :] = part.astype(jnp.bfloat16)
        out = pltpu.make_async_copy(kernel, kernel_hbm, out_sem)
        out.start()
        if cast:
            kernel_ref[...] = kernel[...]
        weights = kernel[...]
    else:
        weights = kernel_ref[...]
    for n in range(blocks):
        part = jnp.dot(taps[n], weights, preferred_element_type=jnp.float32)
        for i in range(high):
            pre_refs[n][i * wide : (i + 1) * wide, :] = part[i * step : i * step + wide]
        spot = (n + 1) % blocks if blocks == 2 else n
        sent_ref[spot] = pre_refs[n][...].astype(jnp.bfloat16)
    if cast or merge:
        out.wait()


def backward_kernel(blocks, others, m, high, classes, scale, step_size, merge, *refs):
    refs = list(refs)
    x_refs, refs = refs[:blocks], refs[blocks:]
    own_refs, refs = refs[:blocks], refs[blocks:]
    other_refs, refs = refs[:others], refs[others:]
    labels_ref, head_hbm, w_hbm, v_hbm, *refs = refs
    if merge:
        peer_hbm, *refs = refs
    half_hbm, sent_hbm, new_v_hbm, *refs = refs
    grads_hbm, refs = refs[:blocks], refs[blocks:]
    flat, spread, beside_ref, slope_ref, wide_ref, head, w, v, sent, grads, sems, out_sems, head_sem, grad_sems, *refs = refs
    wide, step = x_refs[0].shape[0] // high, LINE * m
    rows = high * step
    area = wide // m * high
    chan = w.shape[1]
    depth = w.shape[0] // 3
    parts = [pl.ds(a * depth, depth) for a in range(3)]
    fetch_head = pltpu.make_async_copy(head_hbm, head, head_sem)
    fetch_head.start()
    fetches = []
    for a, p in enumerate(parts):
        fetches.append(
            [
                pltpu.make_async_copy(w_hbm.at[p], w.at[p], sems.at[0, a]),
                pltpu.make_async_copy(v_hbm.at[p], v.at[p], sems.at[1, a]),
            ]
        )
        if merge:
            fetches[a].append(pltpu.make_async_copy(peer_hbm.at[p], refs[0].at[p], refs[1].at[a]))
        for copy in fetches[a]:
            copy.start()
    turn = lax.broadcasted_iota(jnp.int32, (SUB, chan), 0) % m
    pooled = []
    for n in range(blocks):
        pre = own_refs[n][...]
        if others == blocks:
            pre = pre + other_refs[n][0].astype(jnp.float32)
        elif others == 1:
            pre = pre + other_refs[0][n].astype(jnp.float32)
        pre = pre * scale
        sig = jax.nn.sigmoid(pre)
        slope_ref[n] = sig * (1.0 + pre * (1.0 - sig))
        total = jnp.sum((pre * sig).reshape(-1, SUB, chan), axis=0)
        pooled += [jnp.sum(jnp.where(turn == k, total, 0.0), axis=0, keepdims=True) for k in range(m)]
    pooled = (jnp.concatenate(pooled, axis=0) / area).astype(jnp.bfloat16)
    fetch_head.wait()
    logits = lax.dot_general(pooled, head[...], (((1,), (1,)), ((), ())), preferred_element_type=jnp.float32)
    klass = lax.broadcasted_iota(jnp.int32, logits.shape, 1)
    image = lax.broadcasted_iota(jnp.int32, logits.shape, 0)
    logits = jnp.where(klass < classes, logits, -jnp.inf)
    expo = jnp.exp(logits - jnp.max(logits, axis=1, keepdims=True))
    probs = expo / jnp.sum(expo, axis=1, keepdims=True)
    target = jnp.zeros(logits.shape, jnp.int32)
    for n in range(blocks * m):
        target = jnp.where(image == n, labels_ref[0, n], target)
    onehot = (target == klass).astype(jnp.float32)
    dlogits = (LOSS_SCALE * (probs - onehot)).astype(jnp.bfloat16)
    dpooled = jnp.dot(dlogits, head[...], preferred_element_type=jnp.float32) / area
    right = []
    for n in range(blocks):
        tile = jnp.zeros((SUB, chan), jnp.float32)
        for k in range(m):
            tile = jnp.where(turn == k, dpooled[n * m + k : n * m + k + 1], tile)
        slope_ref[n] = (slope_ref[n].reshape(-1, SUB, chan) * tile[None]).reshape(-1, chan)
        for i in range(high):
            wide_ref[i * step : i * step + wide, :] = slope_ref[n, i * wide : (i + 1) * wide, :]
            wide_ref[i * step + wide : (i + 1) * step, :] = jnp.zeros((step - wide, chan), jnp.float32)
        grad = wide_ref[...].astype(jnp.bfloat16)
        grads[n] = grad
        pltpu.make_async_copy(grads.at[n], grads_hbm[n], grad_sems.at[n]).start()
        beside = jnp.concatenate(columns_beside(x_refs[n], flat, spread, m, high), axis=1)
        beside_ref[n * (rows + 2 * step) : (n + 1) * (rows + 2 * step), :] = beside
        lines = []
        for a in range(3):
            pieces = [jnp.zeros((a * step, chan), jnp.bfloat16)] if a else []
            pieces.append(grad)
            pieces += [jnp.zeros(((2 - a) * step, chan), jnp.bfloat16)] if a < 2 else []
            lines.append(jnp.concatenate(pieces, axis=0))
        right.append(jnp.concatenate(lines, axis=1))
    total = lax.dot_general(
        beside_ref[...],
        jnp.concatenate(right, axis=0),
        (((0,), (0,)), ((), ())),
        preferred_element_type=jnp.float32,
    )
    stores = []
    for a, p in enumerate(parts):
        for copy in fetches[a]:
            copy.wait()
        move = total[:, a * chan : (a + 1) * chan] * (step_size * scale / LOSS_SCALE)
        new_v = MOMENTUM * v[p, :] - move
        old = w[p, :]
        if merge:
            old = 0.5 * (old + refs[0][p, :].astype(jnp.float32))
        half = old + MOMENTUM * new_v - move
        sent[p, :] = half.astype(jnp.bfloat16)
        w[p, :] = half
        v[p, :] = new_v
        for k, (src, dst) in enumerate([(sent, sent_hbm), (w, half_hbm), (v, new_v_hbm)]):
            stores.append(pltpu.make_async_copy(src.at[p], dst.at[p], out_sems.at[k, a]))
            stores[-1].start()
    for copy in stores:
        copy.wait()
    for n in range(blocks):
        pltpu.make_async_copy(grads.at[n], grads_hbm[n], grad_sems.at[n]).wait()


def input_gradient_kernel(blocks, m, scale, *refs):
    grad_refs, kernel_ref, out_refs = refs[:blocks], refs[blocks], refs[blocks + 1 :]
    rows, chan = grad_refs[0].shape
    step = LINE * m
    depth = kernel_ref.shape[0] // 3
    share = depth // 3
    edge = jnp.zeros((step, chan), jnp.bfloat16)
    for n in range(blocks):
        grad = jnp.concatenate([edge, grad_refs[n][...], edge], axis=0)
        total = None
        for a in range(3):
            term = lax.dot_general(
                grad[(2 - a) * step : (2 - a) * step + rows],
                kernel_ref[a * depth : (a + 1) * depth, :],
                (((1,), (1,)), ((), ())),
                preferred_element_type=jnp.float32,
            )
            total = term if total is None else total + term
        out = total[:, share : 2 * share]
        out += pltpu.roll(total[:, :share], rows - m, 0)
        out += pltpu.roll(total[:, 2 * share :], m, 0)
        out_refs[n][...] = (out * scale).astype(jnp.bfloat16)


PARAMS = pltpu.CompilerParams(vmem_limit_bytes=30 * 1024 * 1024)
VMEM = pl.BlockSpec(memory_space=pltpu.VMEM)
HBM = pl.BlockSpec(memory_space=pltpu.HBM)
SMEM = pl.BlockSpec(memory_space=pltpu.SMEM)
DMA = pltpu.SemaphoreType.DMA


def f32(*shape, space=jax.ShapeDtypeStruct):
    return space(shape, jnp.float32)


def b16(*shape, space=jax.ShapeDtypeStruct):
    return space(shape, jnp.bfloat16)


def in_hbm(*arrays):
    return [pltpu.with_memory_space_constraint(array, pltpu.HBM) for array in arrays]


def conv_scale(chan):
    return 1.0 / math.sqrt(9 * chan)


def forward(xs, weights, m, high, cast=False, merge=False):
    blocks = len(xs)
    depth, chan = weights[0].shape
    positions, share = xs[0].shape
    outs, out_specs = [f32(positions, chan)] * blocks + [b16(blocks, positions, chan)], [VMEM] * (blocks + 1)
    scratch = [
        pltpu.VMEM((positions, share), jnp.float32),
        pltpu.VMEM(((high + 2) * LINE * m, share), jnp.float32),
    ]
    if cast or merge:
        scratch += [pltpu.VMEM((depth, chan), jnp.float32), pltpu.VMEM((depth, chan), jnp.bfloat16), DMA((3,)), DMA]
        outs = outs + [b16(depth, chan)] * cast + [b16(depth, chan, space=pltpu.HBM)]
        out_specs = out_specs + [VMEM] * cast + [HBM]
    if merge:
        scratch += [pltpu.VMEM((depth, chan), jnp.bfloat16), DMA((3,))]
    return pl.pallas_call(
        partial(forward_kernel, blocks, m, high, cast, merge),
        in_specs=[VMEM] * blocks + [HBM if cast or merge else VMEM] * len(weights),
        out_shape=outs,
        out_specs=out_specs,
        scratch_shapes=scratch,
        compiler_params=PARAMS,
        cost_estimate=pl.CostEstimate(
            flops=2 * blocks * positions * depth * chan, bytes_accessed=4 * depth * chan, transcendentals=0
        ),
        name="forward",
    )(*xs, *(in_hbm(*weights) if cast or merge else weights))


def backward(xs, own, other, labels, head, weights, v, m, high, classes):
    blocks = len(own)
    depth, chan = v.shape
    positions, share = xs[0].shape
    rows = high * LINE * m
    scale = conv_scale(chan)
    step_size = 0.1 * 9 * chan
    merge = len(weights) == 2
    scratch = [
        pltpu.VMEM((positions, share), jnp.float32),
        pltpu.VMEM((rows + 2 * LINE * m, share), jnp.float32),
        pltpu.VMEM((blocks * (rows + 2 * LINE * m), 3 * share), jnp.bfloat16),
        pltpu.VMEM((blocks, positions, chan), jnp.float32),
        pltpu.VMEM((rows, chan), jnp.float32),
        pltpu.VMEM(head.shape, jnp.bfloat16),
        pltpu.VMEM((depth, chan), jnp.float32),
        pltpu.VMEM((depth, chan), jnp.float32),
        pltpu.VMEM((depth, chan), jnp.bfloat16),
        pltpu.VMEM((blocks, rows, chan), jnp.bfloat16),
        DMA((2, 3)),
        DMA((3, 3)),
        DMA,
        DMA((blocks,)),
    ]
    if merge:
        scratch += [pltpu.VMEM((depth, chan), jnp.bfloat16), DMA((3,))]
    return pl.pallas_call(
        partial(backward_kernel, blocks, len(other), m, high, classes, scale, step_size, merge),
        in_specs=[VMEM] * (2 * blocks + len(other)) + [SMEM] + [HBM] * (2 + len(weights)),
        out_shape=[
            f32(depth, chan, space=pltpu.HBM),
            b16(depth, chan, space=pltpu.HBM),
            f32(depth, chan, space=pltpu.HBM),
        ]
        + [b16(rows, chan, space=pltpu.HBM)] * blocks,
        out_specs=[HBM] * (3 + blocks),
        scratch_shapes=scratch,
        compiler_params=PARAMS,
        cost_estimate=pl.CostEstimate(
            flops=2 * blocks * rows * v.size, bytes_accessed=20 * v.size, transcendentals=blocks * rows * chan
        ),
        name="backward",
    )(*xs, *own, *other, labels, *in_hbm(head, weights[0], v, *weights[1:]))


def input_gradient(grads, kernel, m):
    blocks = len(grads)
    rows, chan = grads[0].shape
    share = kernel.shape[0] // 9
    return pl.pallas_call(
        partial(input_gradient_kernel, blocks, m, conv_scale(chan)),
        out_shape=[b16(rows, share)] * blocks,
        compiler_params=PARAMS,
        cost_estimate=pl.CostEstimate(
            flops=2 * blocks * rows * kernel.size, bytes_accessed=2 * kernel.size, transcendentals=0
        ),
        name="input_gradient",
    )(*in_hbm(*grads, kernel))


def local(images, labels, step_index, weights, velocity, head_weight):
    shape = weights.shape
    maps = jnp.transpose(images[:, 0], (0, 2, 3, 1, 4))
    labels = labels[:, 0]
    _, high, wide, m, chan = maps.shape
    share = shape[3]
    members = lax.axis_size("group")
    me = lax.axis_index("group")
    bits = lax.axis_size("replica").bit_length() - 1
    classes = head_weight.shape[0]
    pair = members == 2
    w = weights.reshape(9 * share, chan)
    v = velocity.reshape(9 * share, chan)
    head = jnp.pad(head_weight, ((0, -classes % 128), (0, 0)))

    def flat(part):
        return part.reshape(high * wide * m, share)

    def gossip(turn, pusher, *values):
        select = (step_index[0] + turn) % bits
        return lax.switch(select, [partial(pusher, 1 << position) for position in range(bits)], *values)

    def send_back(parts):
        parts = [part.reshape(high, LINE, m, share)[:, :wide] for part in parts]
        if pair:
            back = shifted(parts[1], "group", 1)
            low = jnp.where(me == 0, parts[0], back)
            top = jnp.where(me == 0, back, parts[0])
            return jnp.concatenate([low, top], axis=3)
        parts = lax.all_to_all(jnp.stack(parts), "group", split_axis=0, concat_axis=0, tiled=True)
        return jnp.concatenate([parts[k] for k in range(members)], axis=3)

    if pair:
        theirs = lax.dynamic_slice_in_dim(maps[0], (1 - me) * share, share, axis=3)
        came = shifted(flat(theirs), "group", 1)
        labels = jnp.concatenate([labels, shifted(labels, "group", 1)], axis=1)
        theirs, rest = lax.optimization_barrier((theirs, maps))
        x_own = flat(lax.dynamic_slice_in_dim(rest[0], me * share, share, axis=3))
        own_a, sent_a, kernel_near, kernel = forward([x_own], [w], m, high, cast=True)
        other_b = shifted(sent_a, "group", 1)
        own_b, sent_b = forward([came], [kernel_near], m, high)
        other_a = shifted(sent_b, "group", 1)
        sent_b, rest = lax.optimization_barrier((sent_b, rest))
        later = [flat(lax.dynamic_slice_in_dim(rest[1], k * share, share, axis=3)) for k in (me, 1 - me)]
        xs, own, other = [x_own, came], [own_a, own_b], [other_a, other_b]
    else:
        split = maps.reshape(ITERS, high, wide, m, members, share)
        split = lax.all_to_all(split, "group", split_axis=4, concat_axis=4, tiled=True)
        labels = lax.all_gather(labels, "group", axis=1, tiled=True)
        later = [flat(split[1, :, :, :, k]) for k in range(members)]
        xs = [flat(split[0, :, :, :, k]) for k in range(members)]
        *own, sent, _, kernel = forward(xs, [w], m, high, cast=True)
        own, other = [lax.psum(part, "group") for part in own], []
    half, sent, v, *grads = backward(xs, own, other, labels[:1], head, [w], v, m, high, classes)

    def first(distance, sent, later):
        peer = shifted(sent, "replica", distance)
        return peer, [later[0], shifted(later[1], "group", 1)] if pair else later

    peer, xs = gossip(0, first, sent, later)
    old_kernel = kernel
    *own, sent, kernel = forward(xs, [half, peer], m, high, merge=True)
    if pair:
        other = [shifted(sent, "group", 1)]
    else:
        own, other = [lax.psum(part, "group") for part in own], []
    grads, sent = lax.optimization_barrier((grads, sent))
    parts = input_gradient(grads, old_kernel, m)
    half, sent, v, *grads = backward(xs, own, other, labels[1:], head, [half, peer], v, m, high, classes)

    def last(distance, sent, parts, grads, kernel):
        peer = shifted(sent, "replica", distance)
        return peer, jnp.stack([send_back(parts), send_back(input_gradient(grads, kernel, m))])

    peer, grads_in = gossip(1, last, sent, parts, grads, kernel)
    w = 0.5 * (half + peer.astype(jnp.float32))
    grads_in = jnp.transpose(grads_in, (0, 3, 1, 2, 4))[:, None]
    return (w.reshape(shape), v.reshape(shape), grads_in)


def solution(mesh):
    return jax.shard_map(
        local,
        mesh=mesh,
        in_specs=(
            P(None, "replica", "group", None, None, None),
            P(None, "replica", "group"),
            P(),
            P("replica", None, None, "group", None),
            P("replica", None, None, "group", None),
            P(),
        ),
        out_specs=(
            P("replica", None, None, "group", None),
            P("replica", None, None, "group", None),
            P(None, "replica", "group", None, None, None),
        ),
        check_vma=False,
    )
```

```python
from functools import partial
import math

import jax
import jax.numpy as jnp
from jax import lax
from jax.experimental import pallas as pl
from jax.experimental.pallas import tpu as pltpu
from jax.sharding import PartitionSpec as P

ITERS = 2

MOMENTUM = 0.9
LOSS_SCALE = 256.0
LINE = 16
SUB = 8


def shifted(x, axis, by):
    length = lax.axis_size(axis)
    return lax.ppermute(x, axis, [(i, (i + by) % length) for i in range(length)])


def line_by_line(dst, src, lines, wide, to, at, start=0):
    for i in range(lines):
        dst[start + i * to : start + i * to + wide, :] = src[i * at : i * at + wide, :]


def columns_beside(x_ref, flat, spread, m, high):
    wide, step = x_ref.shape[0] // high, LINE * m
    flat[...] = x_ref[...].astype(jnp.float32)
    spread[...] = jnp.zeros_like(spread)
    line_by_line(spread, flat, high, wide, step, wide, step)
    rows = spread[...]
    beside = [pltpu.roll(rows, m, 0), rows, pltpu.roll(rows, rows.shape[0] - m, 0)]
    return [part.astype(jnp.bfloat16) for part in beside]


def forward_kernel(blocks, m, high, cast, merge, *refs):
    refs = list(refs)
    x_refs, refs = refs[:blocks], refs[blocks:]
    wide, step = x_refs[0].shape[0] // high, LINE * m
    rows = high * step
    if cast:
        w_hbm, *pre_refs, sent_ref, kernel_ref, kernel_hbm, flat, spread, w, kernel, sems, out_sem = refs
    elif merge:
        w_hbm, peer_hbm, *pre_refs, sent_ref, kernel_hbm, flat, spread, w, kernel, sems, out_sem, peer, peer_sems = refs
    else:
        kernel_ref, *pre_refs, sent_ref, flat, spread = refs
    copies = []
    if cast or merge:
        depth = w.shape[0] // 3
        parts = [pl.ds(a * depth, depth) for a in range(3)]
        copies = [[pltpu.make_async_copy(w_hbm.at[p], w.at[p], sems.at[a])] for a, p in enumerate(parts)]
        if merge:
            for a, p in enumerate(parts):
                copies[a].append(pltpu.make_async_copy(peer_hbm.at[p], peer.at[p], peer_sems.at[a]))
        for part in copies:
            for copy in part:
                copy.start()
    taps = []
    for n in range(blocks):
        beside = columns_beside(x_refs[n], flat, spread, m, high)
        lines = [part[a * step : a * step + rows] for a in range(3) for part in beside]
        taps.append(jnp.concatenate(lines, axis=1))
    if cast or merge:
        for a, p in enumerate(parts):
            for copy in copies[a]:
                copy.wait()
            part = w[p, :]
            if merge:
                part = 0.5 * (part + peer[p, :].astype(jnp.float32))
            kernel[p, :] = part.astype(jnp.bfloat16)
        out = pltpu.make_async_copy(kernel, kernel_hbm, out_sem)
        out.start()
        if cast:
            kernel_ref[...] = kernel[...]
        weights = kernel[...]
    else:
        weights = kernel_ref[...]
    for n in range(blocks):
        part = jnp.dot(taps[n], weights, preferred_element_type=jnp.float32)
        for i in range(high):
            pre_refs[n][i * wide : (i + 1) * wide, :] = part[i * step : i * step + wide]
        spot = (n + 1) % blocks if blocks == 2 else n
        sent_ref[spot] = pre_refs[n][...].astype(jnp.bfloat16)
    if cast or merge:
        out.wait()


def backward_kernel(blocks, others, m, high, classes, scale, step_size, merge, *refs):
    refs = list(refs)
    x_refs, refs = refs[:blocks], refs[blocks:]
    own_refs, refs = refs[:blocks], refs[blocks:]
    other_refs, refs = refs[:others], refs[others:]
    labels_ref, head_hbm, w_hbm, v_hbm, *refs = refs
    if merge:
        peer_hbm, *refs = refs
    half_hbm, sent_hbm, new_v_hbm, *refs = refs
    grads_hbm, refs = refs[:blocks], refs[blocks:]
    flat, spread, beside_ref, slope_ref, wide_ref, head, w, v, sent, grads, sems, out_sems, head_sem, grad_sems, *refs = refs
    wide, step = x_refs[0].shape[0] // high, LINE * m
    rows = high * step
    area = wide // m * high
    chan = w.shape[1]
    depth = w.shape[0] // 3
    parts = [pl.ds(a * depth, depth) for a in range(3)]
    fetch_head = pltpu.make_async_copy(head_hbm, head, head_sem)
    fetch_head.start()
    fetches = []
    for a, p in enumerate(parts):
        fetches.append(
            [
                pltpu.make_async_copy(w_hbm.at[p], w.at[p], sems.at[0, a]),
                pltpu.make_async_copy(v_hbm.at[p], v.at[p], sems.at[1, a]),
            ]
        )
        if merge:
            fetches[a].append(pltpu.make_async_copy(peer_hbm.at[p], refs[0].at[p], refs[1].at[a]))
        for copy in fetches[a]:
            copy.start()
    turn = lax.broadcasted_iota(jnp.int32, (SUB, chan), 0) % m
    pooled = []
    for n in range(blocks):
        pre = own_refs[n][...]
        if others == blocks:
            pre = pre + other_refs[n][0].astype(jnp.float32)
        elif others == 1:
            pre = pre + other_refs[0][n].astype(jnp.float32)
        pre = pre * scale
        sig = jax.nn.sigmoid(pre)
        slope_ref[n] = sig * (1.0 + pre * (1.0 - sig))
        total = jnp.sum((pre * sig).reshape(-1, SUB, chan), axis=0)
        pooled += [jnp.sum(jnp.where(turn == k, total, 0.0), axis=0, keepdims=True) for k in range(m)]
    pooled = (jnp.concatenate(pooled, axis=0) / area).astype(jnp.bfloat16)
    fetch_head.wait()
    logits = lax.dot_general(pooled, head[...], (((1,), (1,)), ((), ())), preferred_element_type=jnp.float32)
    klass = lax.broadcasted_iota(jnp.int32, logits.shape, 1)
    image = lax.broadcasted_iota(jnp.int32, logits.shape, 0)
    logits = jnp.where(klass < classes, logits, -jnp.inf)
    expo = jnp.exp(logits - jnp.max(logits, axis=1, keepdims=True))
    probs = expo / jnp.sum(expo, axis=1, keepdims=True)
    target = jnp.zeros(logits.shape, jnp.int32)
    for n in range(blocks * m):
        target = jnp.where(image == n, labels_ref[0, n], target)
    onehot = (target == klass).astype(jnp.float32)
    dlogits = (LOSS_SCALE * (probs - onehot)).astype(jnp.bfloat16)
    dpooled = jnp.dot(dlogits, head[...], preferred_element_type=jnp.float32) / area
    right = []
    for n in range(blocks):
        tile = jnp.zeros((SUB, chan), jnp.float32)
        for k in range(m):
            tile = jnp.where(turn == k, dpooled[n * m + k : n * m + k + 1], tile)
        slope_ref[n] = (slope_ref[n].reshape(-1, SUB, chan) * tile[None]).reshape(-1, chan)
        for i in range(high):
            wide_ref[i * step : i * step + wide, :] = slope_ref[n, i * wide : (i + 1) * wide, :]
            wide_ref[i * step + wide : (i + 1) * step, :] = jnp.zeros((step - wide, chan), jnp.float32)
        grad = wide_ref[...].astype(jnp.bfloat16)
        grads[n] = grad
        pltpu.make_async_copy(grads.at[n], grads_hbm[n], grad_sems.at[n]).start()
        beside = jnp.concatenate(columns_beside(x_refs[n], flat, spread, m, high), axis=1)
        beside_ref[n * (rows + 2 * step) : (n + 1) * (rows + 2 * step), :] = beside
        lines = []
        for a in range(3):
            pieces = [jnp.zeros((a * step, chan), jnp.bfloat16)] if a else []
            pieces.append(grad)
            pieces += [jnp.zeros(((2 - a) * step, chan), jnp.bfloat16)] if a < 2 else []
            lines.append(jnp.concatenate(pieces, axis=0))
        right.append(jnp.concatenate(lines, axis=1))
    total = lax.dot_general(
        beside_ref[...],
        jnp.concatenate(right, axis=0),
        (((0,), (0,)), ((), ())),
        preferred_element_type=jnp.float32,
    )
    stores = []
    for a, p in enumerate(parts):
        for copy in fetches[a]:
            copy.wait()
        move = total[:, a * chan : (a + 1) * chan] * (step_size * scale / LOSS_SCALE)
        new_v = MOMENTUM * v[p, :] - move
        old = w[p, :]
        if merge:
            old = 0.5 * (old + refs[0][p, :].astype(jnp.float32))
        half = old + MOMENTUM * new_v - move
        sent[p, :] = half.astype(jnp.bfloat16)
        w[p, :] = half
        v[p, :] = new_v
        for k, (src, dst) in enumerate([(sent, sent_hbm), (w, half_hbm), (v, new_v_hbm)]):
            stores.append(pltpu.make_async_copy(src.at[p], dst.at[p], out_sems.at[k, a]))
            stores[-1].start()
    for copy in stores:
        copy.wait()
    for n in range(blocks):
        pltpu.make_async_copy(grads.at[n], grads_hbm[n], grad_sems.at[n]).wait()


def input_gradient_kernel(blocks, m, scale, *refs):
    grad_refs, kernel_ref, out_refs = refs[:blocks], refs[blocks], refs[blocks + 1 :]
    rows, chan = grad_refs[0].shape
    step = LINE * m
    depth = kernel_ref.shape[0] // 3
    share = depth // 3
    edge = jnp.zeros((step, chan), jnp.bfloat16)
    for n in range(blocks):
        grad = jnp.concatenate([edge, grad_refs[n][...], edge], axis=0)
        total = None
        for a in range(3):
            term = lax.dot_general(
                grad[(2 - a) * step : (2 - a) * step + rows],
                kernel_ref[a * depth : (a + 1) * depth, :],
                (((1,), (1,)), ((), ())),
                preferred_element_type=jnp.float32,
            )
            total = term if total is None else total + term
        out = total[:, share : 2 * share]
        out += pltpu.roll(total[:, :share], rows - m, 0)
        out += pltpu.roll(total[:, 2 * share :], m, 0)
        out_refs[n][...] = (out * scale).astype(jnp.bfloat16)


PARAMS = pltpu.CompilerParams(vmem_limit_bytes=30 * 1024 * 1024)
VMEM = pl.BlockSpec(memory_space=pltpu.VMEM)
HBM = pl.BlockSpec(memory_space=pltpu.HBM)
SMEM = pl.BlockSpec(memory_space=pltpu.SMEM)
DMA = pltpu.SemaphoreType.DMA


def f32(*shape, space=jax.ShapeDtypeStruct):
    return space(shape, jnp.float32)


def b16(*shape, space=jax.ShapeDtypeStruct):
    return space(shape, jnp.bfloat16)


def in_hbm(*arrays):
    return [pltpu.with_memory_space_constraint(array, pltpu.HBM) for array in arrays]


def conv_scale(chan):
    return 1.0 / math.sqrt(9 * chan)


def forward(xs, weights, m, high, cast=False, merge=False):
    blocks = len(xs)
    depth, chan = weights[0].shape
    positions, share = xs[0].shape
    outs, out_specs = [f32(positions, chan)] * blocks + [b16(blocks, positions, chan)], [VMEM] * (blocks + 1)
    scratch = [
        pltpu.VMEM((positions, share), jnp.float32),
        pltpu.VMEM(((high + 2) * LINE * m, share), jnp.float32),
    ]
    if cast or merge:
        scratch += [pltpu.VMEM((depth, chan), jnp.float32), pltpu.VMEM((depth, chan), jnp.bfloat16), DMA((3,)), DMA]
        outs = outs + [b16(depth, chan)] * cast + [b16(depth, chan, space=pltpu.HBM)]
        out_specs = out_specs + [VMEM] * cast + [HBM]
    if merge:
        scratch += [pltpu.VMEM((depth, chan), jnp.bfloat16), DMA((3,))]
    return pl.pallas_call(
        partial(forward_kernel, blocks, m, high, cast, merge),
        in_specs=[VMEM] * blocks + [HBM if cast or merge else VMEM] * len(weights),
        out_shape=outs,
        out_specs=out_specs,
        scratch_shapes=scratch,
        compiler_params=PARAMS,
        cost_estimate=pl.CostEstimate(
            flops=2 * blocks * positions * depth * chan, bytes_accessed=4 * depth * chan, transcendentals=0
        ),
        name="forward",
    )(*xs, *(in_hbm(*weights) if cast or merge else weights))


def backward(xs, own, other, labels, head, weights, v, m, high, classes):
    blocks = len(own)
    depth, chan = v.shape
    positions, share = xs[0].shape
    rows = high * LINE * m
    scale = conv_scale(chan)
    step_size = 0.1 * 9 * chan
    merge = len(weights) == 2
    scratch = [
        pltpu.VMEM((positions, share), jnp.float32),
        pltpu.VMEM((rows + 2 * LINE * m, share), jnp.float32),
        pltpu.VMEM((blocks * (rows + 2 * LINE * m), 3 * share), jnp.bfloat16),
        pltpu.VMEM((blocks, positions, chan), jnp.float32),
        pltpu.VMEM((rows, chan), jnp.float32),
        pltpu.VMEM(head.shape, jnp.bfloat16),
        pltpu.VMEM((depth, chan), jnp.float32),
        pltpu.VMEM((depth, chan), jnp.float32),
        pltpu.VMEM((depth, chan), jnp.bfloat16),
        pltpu.VMEM((blocks, rows, chan), jnp.bfloat16),
        DMA((2, 3)),
        DMA((3, 3)),
        DMA,
        DMA((blocks,)),
    ]
    if merge:
        scratch += [pltpu.VMEM((depth, chan), jnp.bfloat16), DMA((3,))]
    return pl.pallas_call(
        partial(backward_kernel, blocks, len(other), m, high, classes, scale, step_size, merge),
        in_specs=[VMEM] * (2 * blocks + len(other)) + [SMEM] + [HBM] * (2 + len(weights)),
        out_shape=[
            f32(depth, chan, space=pltpu.HBM),
            b16(depth, chan, space=pltpu.HBM),
            f32(depth, chan, space=pltpu.HBM),
        ]
        + [b16(rows, chan, space=pltpu.HBM)] * blocks,
        out_specs=[HBM] * (3 + blocks),
        scratch_shapes=scratch,
        compiler_params=PARAMS,
        cost_estimate=pl.CostEstimate(
            flops=2 * blocks * rows * v.size, bytes_accessed=20 * v.size, transcendentals=blocks * rows * chan
        ),
        name="backward",
    )(*xs, *own, *other, labels, *in_hbm(head, weights[0], v, *weights[1:]))


def input_gradient(grads, kernel, m):
    blocks = len(grads)
    rows, chan = grads[0].shape
    share = kernel.shape[0] // 9
    return pl.pallas_call(
        partial(input_gradient_kernel, blocks, m, conv_scale(chan)),
        out_shape=[b16(rows, share)] * blocks,
        compiler_params=PARAMS,
        cost_estimate=pl.CostEstimate(
            flops=2 * blocks * rows * kernel.size, bytes_accessed=2 * kernel.size, transcendentals=0
        ),
        name="input_gradient",
    )(*in_hbm(*grads, kernel))


def local(images, labels, step_index, weights, velocity, head_weight):
    shape = weights.shape
    maps = jnp.transpose(images[:, 0], (0, 2, 3, 1, 4))
    labels = labels[:, 0]
    _, high, wide, m, chan = maps.shape
    share = shape[3]
    members = lax.axis_size("group")
    me = lax.axis_index("group")
    bits = lax.axis_size("replica").bit_length() - 1
    classes = head_weight.shape[0]
    pair = members == 2
    w = weights.reshape(9 * share, chan)
    v = velocity.reshape(9 * share, chan)
    head = jnp.pad(head_weight, ((0, -classes % 128), (0, 0)))

    def flat(part):
        return part.reshape(high * wide * m, share)

    def gossip(turn, pusher, *values):
        select = (step_index[0] + turn) % bits
        return lax.switch(select, [partial(pusher, 1 << position) for position in range(bits)], *values)

    def send_back(parts):
        parts = [part.reshape(high, LINE, m, share)[:, :wide] for part in parts]
        if pair:
            back = shifted(parts[1], "group", 1)
            low = jnp.where(me == 0, parts[0], back)
            top = jnp.where(me == 0, back, parts[0])
            return jnp.concatenate([low, top], axis=3)
        parts = lax.all_to_all(jnp.stack(parts), "group", split_axis=0, concat_axis=0, tiled=True)
        return jnp.concatenate([parts[k] for k in range(members)], axis=3)

    if pair:
        theirs = lax.dynamic_slice_in_dim(maps[0], (1 - me) * share, share, axis=3)
        came = shifted(flat(theirs), "group", 1)
        labels = jnp.concatenate([labels, shifted(labels, "group", 1)], axis=1)
        theirs, rest = lax.optimization_barrier((theirs, maps))
        x_own = flat(lax.dynamic_slice_in_dim(rest[0], me * share, share, axis=3))
        own_a, sent_a, kernel_near, kernel = forward([x_own], [w], m, high, cast=True)
        other_b = shifted(sent_a, "group", 1)
        own_b, sent_b = forward([came], [kernel_near], m, high)
        other_a = shifted(sent_b, "group", 1)
        sent_b, rest = lax.optimization_barrier((sent_b, rest))
        later = [flat(lax.dynamic_slice_in_dim(rest[1], k * share, share, axis=3)) for k in (me, 1 - me)]
        xs, own, other = [x_own, came], [own_a, own_b], [other_a, other_b]
    else:
        split = maps.reshape(ITERS, high, wide, m, members, share)
        split = lax.all_to_all(split, "group", split_axis=4, concat_axis=4, tiled=True)
        labels = lax.all_gather(labels, "group", axis=1, tiled=True)
        later = [flat(split[1, :, :, :, k]) for k in range(members)]
        xs = [flat(split[0, :, :, :, k]) for k in range(members)]
        *own, sent, _, kernel = forward(xs, [w], m, high, cast=True)
        own, other = [lax.psum(part, "group") for part in own], []
    half, sent, v, *grads = backward(xs, own, other, labels[:1], head, [w], v, m, high, classes)

    def rest(distance, half, sent, v, grads, later, kernel, labels, head):
        second = max(distance * 2 % (1 << bits), 1)
        peer = shifted(sent, "replica", distance)
        xs = [later[0], shifted(later[1], "group", 1)] if pair else later
        old_kernel = kernel
        *own, sent, kernel = forward(xs, [half, peer], m, high, merge=True)
        if pair:
            other = [shifted(sent, "group", 1)]
        else:
            own, other = [lax.psum(part, "group") for part in own], []
        grads, sent = lax.optimization_barrier((grads, sent))
        parts = input_gradient(grads, old_kernel, m)
        half, sent, v, *grads = backward(xs, own, other, labels[1:], head, [half, peer], v, m, high, classes)
        peer = shifted(sent, "replica", second)
        grads_in = jnp.stack([send_back(parts), send_back(input_gradient(grads, kernel, m))])
        w = 0.5 * (half + peer.astype(jnp.float32))
        return w, v, grads_in

    w, v, grads_in = gossip(0, rest, half, sent, v, grads, later, kernel, labels, head)
    grads_in = jnp.transpose(grads_in, (0, 3, 1, 2, 4))[:, None]
    return (w.reshape(shape), v.reshape(shape), grads_in)


def solution(mesh):
    return jax.shard_map(
        local,
        mesh=mesh,
        in_specs=(
            P(None, "replica", "group", None, None, None),
            P(None, "replica", "group"),
            P(),
            P("replica", None, None, "group", None),
            P("replica", None, None, "group", None),
            P(),
        ),
        out_specs=(
            P("replica", None, None, "group", None),
            P("replica", None, None, "group", None),
            P(None, "replica", "group", None, None, None),
        ),
        check_vma=False,
    )
```

```python
from functools import partial
import math

import jax
import jax.numpy as jnp
from jax import lax
from jax.experimental import pallas as pl
from jax.experimental.pallas import tpu as pltpu
from jax.sharding import PartitionSpec as P

ITERS = 2

MOMENTUM = 0.9
LOSS_SCALE = 256.0
LINE = 16
SUB = 8


def shifted(x, axis, by):
    length = lax.axis_size(axis)
    return lax.ppermute(x, axis, [(i, (i + by) % length) for i in range(length)])


def line_by_line(dst, src, lines, wide, to, at, start=0):
    for i in range(lines):
        dst[start + i * to : start + i * to + wide, :] = src[i * at : i * at + wide, :]


def columns_beside(x_ref, flat, spread, m, high):
    wide, step = x_ref.shape[0] // high, LINE * m
    flat[...] = x_ref[...].astype(jnp.float32)
    spread[...] = jnp.zeros_like(spread)
    line_by_line(spread, flat, high, wide, step, wide, step)
    rows = spread[...]
    beside = [pltpu.roll(rows, m, 0), rows, pltpu.roll(rows, rows.shape[0] - m, 0)]
    return [part.astype(jnp.bfloat16) for part in beside]


def forward_kernel(blocks, m, high, merge, *refs):
    refs = list(refs)
    x_refs, refs = refs[:blocks], refs[blocks:]
    wide, step = x_refs[0].shape[0] // high, LINE * m
    rows = high * step
    if merge:
        half_ref, peer_ref, *pre_refs, sent_ref, kernel_ref, flat, spread = refs
        merged = 0.5 * (half_ref[...] + peer_ref[...].astype(jnp.float32))
        kernel_ref[...] = merged.astype(jnp.bfloat16)
    else:
        kernel_ref, *pre_refs, sent_ref, flat, spread = refs
    for n in range(blocks):
        beside = columns_beside(x_refs[n], flat, spread, m, high)
        lines = [part[a * step : a * step + rows] for a in range(3) for part in beside]
        part = jnp.dot(jnp.concatenate(lines, axis=1), kernel_ref[...], preferred_element_type=jnp.float32)
        for i in range(high):
            pre_refs[n][i * wide : (i + 1) * wide, :] = part[i * step : i * step + wide]
        spot = (n + 1) % blocks if blocks == 2 else n
        sent_ref[spot] = pre_refs[n][...].astype(jnp.bfloat16)


def backward_kernel(blocks, others, m, high, classes, scale, step_size, merge, stash, *refs):
    refs = list(refs)
    x_refs, refs = refs[:blocks], refs[blocks:]
    own_refs, refs = refs[:blocks], refs[blocks:]
    other_refs, refs = refs[:others], refs[others:]
    labels_ref, head, w_ref, v_ref, *refs = refs
    if merge:
        peer_ref, *refs = refs
    sent, half_out, v_out, *refs = refs
    grads_out, refs = refs[:blocks], refs[blocks:]
    flat, spread, beside_ref, slope_ref, wide_ref, *refs = refs
    if stash:
        half_ref, new_v_ref, grads, sems, grad_sems = refs
        grad_refs = [grads.at[n] for n in range(blocks)]
    else:
        half_ref, new_v_ref, grad_refs = half_out, v_out, grads_out
    wide, step = x_refs[0].shape[0] // high, LINE * m
    rows = high * step
    area = wide // m * high
    depth, chan = w_ref.shape[0] // 3, w_ref.shape[1]
    parts = [pl.ds(a * depth, depth) for a in range(3)]
    stores = []
    turn = lax.broadcasted_iota(jnp.int32, (SUB, chan), 0) % m
    pooled = []
    for n in range(blocks):
        pre = own_refs[n][...]
        if others == blocks:
            pre = pre + other_refs[n][0].astype(jnp.float32)
        elif others == 1:
            pre = pre + other_refs[0][n].astype(jnp.float32)
        pre = pre * scale
        sig = jax.nn.sigmoid(pre)
        slope_ref[n] = sig * (1.0 + pre * (1.0 - sig))
        total = jnp.sum((pre * sig).reshape(-1, SUB, chan), axis=0)
        pooled += [jnp.sum(jnp.where(turn == k, total, 0.0), axis=0, keepdims=True) for k in range(m)]
    pooled = (jnp.concatenate(pooled, axis=0) / area).astype(jnp.bfloat16)
    logits = lax.dot_general(pooled, head[...], (((1,), (1,)), ((), ())), preferred_element_type=jnp.float32)
    klass = lax.broadcasted_iota(jnp.int32, logits.shape, 1)
    image = lax.broadcasted_iota(jnp.int32, logits.shape, 0)
    logits = jnp.where(klass < classes, logits, -jnp.inf)
    expo = jnp.exp(logits - jnp.max(logits, axis=1, keepdims=True))
    probs = expo / jnp.sum(expo, axis=1, keepdims=True)
    target = jnp.zeros(logits.shape, jnp.int32)
    for n in range(blocks * m):
        target = jnp.where(image == n, labels_ref[0, n], target)
    onehot = (target == klass).astype(jnp.float32)
    dlogits = (LOSS_SCALE * (probs - onehot)).astype(jnp.bfloat16)
    dpooled = jnp.dot(dlogits, head[...], preferred_element_type=jnp.float32) / area
    right = []
    for n in range(blocks):
        tile = jnp.zeros((SUB, chan), jnp.float32)
        for k in range(m):
            tile = jnp.where(turn == k, dpooled[n * m + k : n * m + k + 1], tile)
        slope_ref[n] = (slope_ref[n].reshape(-1, SUB, chan) * tile[None]).reshape(-1, chan)
        for i in range(high):
            wide_ref[i * step : i * step + wide, :] = slope_ref[n, i * wide : (i + 1) * wide, :]
            wide_ref[i * step + wide : (i + 1) * step, :] = jnp.zeros((step - wide, chan), jnp.float32)
        grad = wide_ref[...].astype(jnp.bfloat16)
        grad_refs[n][...] = grad
        if stash:
            stores.append(pltpu.make_async_copy(grad_refs[n], grads_out[n], grad_sems.at[n]))
            stores[-1].start()
        beside = jnp.concatenate(columns_beside(x_refs[n], flat, spread, m, high), axis=1)
        beside_ref[n * (rows + 2 * step) : (n + 1) * (rows + 2 * step), :] = beside
        lines = []
        for a in range(3):
            pieces = [jnp.zeros((a * step, chan), jnp.bfloat16)] if a else []
            pieces.append(grad)
            pieces += [jnp.zeros(((2 - a) * step, chan), jnp.bfloat16)] if a < 2 else []
            lines.append(jnp.concatenate(pieces, axis=0))
        right.append(jnp.concatenate(lines, axis=1))
    total = lax.dot_general(
        beside_ref[...],
        jnp.concatenate(right, axis=0),
        (((0,), (0,)), ((), ())),
        preferred_element_type=jnp.float32,
    )
    for a, p in enumerate(parts):
        move = total[:, a * chan : (a + 1) * chan] * (step_size * scale / LOSS_SCALE)
        new_v = MOMENTUM * v_ref[p, :] - move
        old = w_ref[p, :]
        if merge:
            old = 0.5 * (old + peer_ref[p, :].astype(jnp.float32))
        half = old + MOMENTUM * new_v - move
        sent[p, :] = half.astype(jnp.bfloat16)
        half_ref[p, :] = half
        new_v_ref[p, :] = new_v
        if stash:
            for k, (src, dst) in enumerate([(half_ref, half_out), (new_v_ref, v_out)]):
                stores.append(pltpu.make_async_copy(src.at[p], dst.at[p], sems.at[k, a]))
                stores[-1].start()
    for copy in stores:
        copy.wait()


def input_gradient_kernel(blocks, m, scale, *refs):
    grad_refs, kernel_ref, out_refs = refs[:blocks], refs[blocks], refs[blocks + 1 :]
    rows, chan = grad_refs[0].shape
    step = LINE * m
    depth = kernel_ref.shape[0] // 3
    share = depth // 3
    edge = jnp.zeros((step, chan), jnp.bfloat16)
    for n in range(blocks):
        grad = jnp.concatenate([edge, grad_refs[n][...], edge], axis=0)
        total = None
        for a in range(3):
            term = lax.dot_general(
                grad[(2 - a) * step : (2 - a) * step + rows],
                kernel_ref[a * depth : (a + 1) * depth, :],
                (((1,), (1,)), ((), ())),
                preferred_element_type=jnp.float32,
            )
            total = term if total is None else total + term
        out = total[:, share : 2 * share]
        out += pltpu.roll(total[:, :share], rows - m, 0)
        out += pltpu.roll(total[:, 2 * share :], m, 0)
        out_refs[n][...] = (out * scale).astype(jnp.bfloat16)


def split_kernel(turn, share, maps, mine, theirs, sems):
    me = lax.axis_index("group")
    copies = []
    for k, (dst, spot) in enumerate([(theirs, 1 - me), (mine, me)]):
        channels = pl.ds(pl.multiple_of(spot * share, share), share)
        copies.append(pltpu.make_async_copy(maps.at[turn, :, :, :, channels], dst, sems.at[k]))
        copies[-1].start()
    for copy in copies:
        copy.wait()


def finish_kernel(pair, high, wide, share, *refs):
    half_ref, peer_ref, *refs = refs
    if pair:
        *blocks, w_hbm, grads_hbm, w, sems, out_sems = refs
        stores = []
        spots = [lax.axis_index("group"), 1 - lax.axis_index("group")]
        for k, block in enumerate(blocks):
            channels = pl.ds(pl.multiple_of(spots[k % 2] * share, share), share)
            src = block.at[pl.ds(0, high), pl.ds(0, wide)]
            stores.append(pltpu.make_async_copy(src, grads_hbm.at[k // 2, :, :, :, channels], sems.at[k]))
            stores[-1].start()
    else:
        (w_hbm, w, out_sems), stores = refs, []
    depth = w.shape[0] // 3
    for a in range(3):
        p = pl.ds(a * depth, depth)
        w[p, :] = 0.5 * (half_ref[p, :] + peer_ref[p, :].astype(jnp.float32))
        stores.append(pltpu.make_async_copy(w.at[p], w_hbm.at[p], out_sems.at[a]))
        stores[-1].start()
    for copy in stores:
        copy.wait()


PARAMS = pltpu.CompilerParams(vmem_limit_bytes=24 * 1024 * 1024)
VMEM = pl.BlockSpec(memory_space=pltpu.VMEM)
HBM = pl.BlockSpec(memory_space=pltpu.HBM)
SMEM = pl.BlockSpec(memory_space=pltpu.SMEM)
DMA = pltpu.SemaphoreType.DMA


def f32(*shape, space=jax.ShapeDtypeStruct):
    return space(shape, jnp.float32)


def b16(*shape, space=jax.ShapeDtypeStruct):
    return space(shape, jnp.bfloat16)


def conv_scale(chan):
    return 1.0 / math.sqrt(9 * chan)


def forward(xs, weights, m, high):
    blocks = len(xs)
    depth, chan = weights[0].shape
    positions, share = xs[0].shape
    merge = len(weights) == 2
    return pl.pallas_call(
        partial(forward_kernel, blocks, m, high, merge),
        out_shape=[f32(positions, chan)] * blocks + [b16(blocks, positions, chan)] + [b16(depth, chan)] * merge,
        scratch_shapes=[
            pltpu.VMEM((positions, share), jnp.float32),
            pltpu.VMEM(((high + 2) * LINE * m, share), jnp.float32),
        ],
        compiler_params=PARAMS,
        cost_estimate=pl.CostEstimate(
            flops=2 * blocks * positions * depth * chan, bytes_accessed=4 * depth * chan, transcendentals=0
        ),
        name="forward",
    )(*xs, *weights)


def backward(xs, own, other, labels, head, weights, v, m, high, classes, stash=False):
    blocks = len(own)
    depth, chan = v.shape
    positions, share = xs[0].shape
    rows = high * LINE * m
    scale = conv_scale(chan)
    step_size = 0.1 * 9 * chan
    merge = len(weights) == 2
    scratch = [
        pltpu.VMEM((positions, share), jnp.float32),
        pltpu.VMEM((rows + 2 * LINE * m, share), jnp.float32),
        pltpu.VMEM((blocks * (rows + 2 * LINE * m), 3 * share), jnp.bfloat16),
        pltpu.VMEM((blocks, positions, chan), jnp.float32),
        pltpu.VMEM((rows, chan), jnp.float32),
    ]
    if stash:
        scratch += [
            pltpu.VMEM((depth, chan), jnp.float32),
            pltpu.VMEM((depth, chan), jnp.float32),
            pltpu.VMEM((blocks, rows, chan), jnp.bfloat16),
            DMA((2, 3)),
            DMA((blocks,)),
        ]
    place = {"space": pltpu.HBM} if stash else {}
    return pl.pallas_call(
        partial(backward_kernel, blocks, len(other), m, high, classes, scale, step_size, merge, stash),
        in_specs=[VMEM] * (2 * blocks + len(other)) + [SMEM] + [VMEM] * (2 + len(weights)),
        out_shape=[b16(depth, chan)]
        + [f32(depth, chan, **place)] * 2
        + [b16(rows, chan, **place)] * blocks,
        out_specs=[VMEM] + [HBM if stash else VMEM] * (2 + blocks),
        scratch_shapes=scratch,
        compiler_params=PARAMS,
        cost_estimate=pl.CostEstimate(
            flops=2 * blocks * rows * v.size, bytes_accessed=20 * v.size, transcendentals=blocks * rows * chan
        ),
        name="backward",
    )(*xs, *own, *other, labels, head, weights[0], v, *weights[1:])


def input_gradient(grads, kernel, m):
    blocks = len(grads)
    rows, chan = grads[0].shape
    share = kernel.shape[0] // 9
    return pl.pallas_call(
        partial(input_gradient_kernel, blocks, m, conv_scale(chan)),
        out_shape=[b16(rows, share)] * blocks,
        compiler_params=PARAMS,
        cost_estimate=pl.CostEstimate(flops=1, bytes_accessed=1, transcendentals=0),
        name="input_gradient",
    )(*grads, kernel)


def split(maps, turn):
    _, high, wide, m, chan = maps.shape
    share = chan // 2
    mine, theirs = pl.pallas_call(
        partial(split_kernel, turn, share),
        in_specs=[pl.BlockSpec(memory_space=pl.ANY)],
        out_shape=[b16(high, wide, m, share)] * 2,
        out_specs=[pl.BlockSpec(memory_space=pl.ANY)] * 2,
        scratch_shapes=[DMA((2,))],
        compiler_params=PARAMS,
        cost_estimate=pl.CostEstimate(flops=1, bytes_accessed=1, transcendentals=0),
        name="split",
    )(maps)
    return mine.reshape(-1, share), theirs.reshape(-1, share)


def finish(half, peer, blocks, high, wide, m):
    depth, chan = half.shape
    share = depth // 9
    pair = len(blocks) > 0
    blocks = [block.reshape(high, LINE, m, share) for block in blocks]
    grads = [b16(ITERS, high, wide, m, chan, space=pltpu.HBM)] if pair else []
    outs = pl.pallas_call(
        partial(finish_kernel, pair, high, wide, share),
        in_specs=[VMEM] * 2 + [pl.BlockSpec(memory_space=pl.ANY)] * len(blocks),
        out_shape=[f32(depth, chan, space=pltpu.HBM)] + grads,
        out_specs=[HBM] * (1 + pair),
        scratch_shapes=[pltpu.VMEM((depth, chan), jnp.float32)] + [DMA((2 * ITERS,))] * pair + [DMA((3,))],
        compiler_params=PARAMS,
        cost_estimate=pl.CostEstimate(flops=1, bytes_accessed=1, transcendentals=0),
        name="finish",
    )(half, peer, *blocks)
    return outs if pair else (outs[0], None)


def local(images, labels, step_index, weights, velocity, head_weight):
    shape = weights.shape
    maps = jnp.transpose(images[:, 0], (0, 2, 3, 1, 4))
    labels = labels[:, 0]
    _, high, wide, m, chan = maps.shape
    share = shape[3]
    members = lax.axis_size("group")
    bits = lax.axis_size("replica").bit_length() - 1
    classes = head_weight.shape[0]
    pair = members == 2
    w = weights.reshape(9 * share, chan)
    v = velocity.reshape(9 * share, chan)
    head = jnp.pad(head_weight, ((0, -classes % 128), (0, 0)))

    def flat(part):
        return part.reshape(high * wide * m, share)

    def send_back(parts):
        parts = [part.reshape(high, LINE, m, share)[:, :wide] for part in parts]
        parts = lax.all_to_all(jnp.stack(parts), "group", split_axis=0, concat_axis=0, tiled=True)
        return jnp.concatenate([parts[k] for k in range(members)], axis=3)

    if pair:
        mine, theirs = split(maps, 0)
        came = shifted(theirs, "group", 1)
        labels = jnp.concatenate([labels, shifted(labels, "group", 1)], axis=1)
        xs = [mine, came]
    else:
        shares = maps.reshape(ITERS, high, wide, m, members, share)
        shares = lax.all_to_all(shares, "group", split_axis=4, concat_axis=4, tiled=True)
        labels = lax.all_gather(labels, "group", axis=1, tiled=True)
        xs, later = [[flat(shares[t, :, :, :, k]) for k in range(members)] for t in range(ITERS)]

    def add_up(own, sent):
        if pair:
            return own, [shifted(sent, "group", 1)]
        return [lax.psum(part, "group") for part in own], []

    *own, sent = forward(xs, [w.astype(jnp.bfloat16)], m, high)
    own, other = add_up(own, sent)
    sent, half, v, *grads = backward(xs, own, other, labels[:1], head, [w], v, m, high, classes, stash=True)

    def rest(distance, second, half, sent, v, grads, w, labels, head):
        peer = shifted(sent, "replica", distance)
        if pair:
            mine, theirs = split(maps, 1)
            xs = [mine, shifted(theirs, "group", 1)]
        else:
            xs = later
        *own, sent, kernel = forward(xs, [half, peer], m, high)
        own, other = add_up(own, sent)
        grads, w, sent = lax.optimization_barrier((grads, w, sent))
        parts = input_gradient(grads, w.astype(jnp.bfloat16), m)
        sent, half, v, *grads = backward(xs, own, other, labels[1:], head, [half, peer], v, m, high, classes)
        if pair:
            parts, sent = lax.optimization_barrier((parts, sent))
        peer = shifted(sent, "replica", second)
        last = input_gradient(grads, kernel, m)
        if pair:
            blocks = [parts[0], shifted(parts[1], "group", 1), last[0], shifted(last[1], "group", 1)]
            w, grads_in = finish(half, peer, blocks, high, wide, m)
        else:
            w, _ = finish(half, peer, [], high, wide, m)
            grads_in = jnp.stack([send_back(parts), send_back(last)])
        return w, v, grads_in

    branches = [partial(rest, 1 << k, 1 << (k + 1) % bits) for k in range(bits)]
    w, v, grads_in = lax.switch(step_index[0] % bits, branches, half, sent, v, grads, w, labels, head)
    grads_in = jnp.transpose(grads_in, (0, 3, 1, 2, 4))[:, None]
    return (w.reshape(shape), v.reshape(shape), grads_in)


def solution(mesh):
    return jax.shard_map(
        local,
        mesh=mesh,
        in_specs=(
            P(None, "replica", "group", None, None, None),
            P(None, "replica", "group"),
            P(),
            P("replica", None, None, "group", None),
            P("replica", None, None, "group", None),
            P(),
        ),
        out_specs=(
            P("replica", None, None, "group", None),
            P("replica", None, None, "group", None),
            P(None, "replica", "group", None, None, None),
        ),
        check_vma=False,
    )
```

```python
from functools import partial
import math

import jax
import jax.numpy as jnp
from jax import lax
from jax.experimental import pallas as pl
from jax.experimental.pallas import tpu as pltpu
from jax.sharding import PartitionSpec as P

ITERS = 2

MOMENTUM = 0.9
LOSS_SCALE = 256.0
LINE = 16
SUB = 8


def shifted(x, axis, by):
    length = lax.axis_size(axis)
    return lax.ppermute(x, axis, [(i, (i + by) % length) for i in range(length)])


def line_by_line(dst, src, lines, wide, to, at, start=0):
    for i in range(lines):
        dst[start + i * to : start + i * to + wide, :] = src[i * at : i * at + wide, :]


def columns_beside(x_ref, flat, spread, m, high):
    wide, step = x_ref.shape[0] // high, LINE * m
    flat[...] = x_ref[...].astype(jnp.float32)
    spread[...] = jnp.zeros_like(spread)
    line_by_line(spread, flat, high, wide, step, wide, step)
    rows = spread[...]
    beside = [pltpu.roll(rows, m, 0), rows, pltpu.roll(rows, rows.shape[0] - m, 0)]
    return [part.astype(jnp.bfloat16) for part in beside]


def forward_kernel(blocks, m, high, merge, *refs):
    refs = list(refs)
    x_refs, refs = refs[:blocks], refs[blocks:]
    wide, step = x_refs[0].shape[0] // high, LINE * m
    rows = high * step
    if merge:
        half_ref, peer_ref, *pre_refs, sent_ref, kernel_ref, flat, spread = refs
        merged = 0.5 * (half_ref[...] + peer_ref[...].astype(jnp.float32))
        kernel_ref[...] = merged.astype(jnp.bfloat16)
    else:
        kernel_ref, *pre_refs, sent_ref, flat, spread = refs
    for n in range(blocks):
        beside = columns_beside(x_refs[n], flat, spread, m, high)
        lines = [part[a * step : a * step + rows] for a in range(3) for part in beside]
        part = jnp.dot(jnp.concatenate(lines, axis=1), kernel_ref[...], preferred_element_type=jnp.float32)
        for i in range(high):
            pre_refs[n][i * wide : (i + 1) * wide, :] = part[i * step : i * step + wide]
        spot = (n + 1) % blocks if blocks == 2 else n
        sent_ref[spot] = pre_refs[n][...].astype(jnp.bfloat16)


def backward_kernel(blocks, others, m, high, classes, scale, step_size, merge, *refs):
    refs = list(refs)
    x_refs, refs = refs[:blocks], refs[blocks:]
    own_refs, refs = refs[:blocks], refs[blocks:]
    other_refs, refs = refs[:others], refs[others:]
    labels_ref, head, w_ref, v_ref, *refs = refs
    if merge:
        peer_ref, *refs = refs
    sent, half_ref, new_v_ref, *refs = refs
    grad_refs, refs = refs[:blocks], refs[blocks:]
    flat, spread, beside_ref, slope_ref, wide_ref = refs
    wide, step = x_refs[0].shape[0] // high, LINE * m
    rows = high * step
    area = wide // m * high
    depth, chan = w_ref.shape[0] // 3, w_ref.shape[1]
    parts = [pl.ds(a * depth, depth) for a in range(3)]
    turn = lax.broadcasted_iota(jnp.int32, (SUB, chan), 0) % m
    pooled = []
    for n in range(blocks):
        pre = own_refs[n][...]
        if others == blocks:
            pre = pre + other_refs[n][0].astype(jnp.float32)
        elif others == 1:
            pre = pre + other_refs[0][n].astype(jnp.float32)
        pre = pre * scale
        sig = jax.nn.sigmoid(pre)
        slope_ref[n] = sig * (1.0 + pre * (1.0 - sig))
        total = jnp.sum((pre * sig).reshape(-1, SUB, chan), axis=0)
        pooled += [jnp.sum(jnp.where(turn == k, total, 0.0), axis=0, keepdims=True) for k in range(m)]
    pooled = (jnp.concatenate(pooled, axis=0) / area).astype(jnp.bfloat16)
    logits = lax.dot_general(pooled, head[...], (((1,), (1,)), ((), ())), preferred_element_type=jnp.float32)
    klass = lax.broadcasted_iota(jnp.int32, logits.shape, 1)
    image = lax.broadcasted_iota(jnp.int32, logits.shape, 0)
    logits = jnp.where(klass < classes, logits, -jnp.inf)
    expo = jnp.exp(logits - jnp.max(logits, axis=1, keepdims=True))
    probs = expo / jnp.sum(expo, axis=1, keepdims=True)
    target = jnp.zeros(logits.shape, jnp.int32)
    for n in range(blocks * m):
        target = jnp.where(image == n, labels_ref[0, n], target)
    onehot = (target == klass).astype(jnp.float32)
    dlogits = (LOSS_SCALE * (probs - onehot)).astype(jnp.bfloat16)
    dpooled = jnp.dot(dlogits, head[...], preferred_element_type=jnp.float32) / area
    right = []
    for n in range(blocks):
        tile = jnp.zeros((SUB, chan), jnp.float32)
        for k in range(m):
            tile = jnp.where(turn == k, dpooled[n * m + k : n * m + k + 1], tile)
        slope_ref[n] = (slope_ref[n].reshape(-1, SUB, chan) * tile[None]).reshape(-1, chan)
        for i in range(high):
            wide_ref[i * step : i * step + wide, :] = slope_ref[n, i * wide : (i + 1) * wide, :]
            wide_ref[i * step + wide : (i + 1) * step, :] = jnp.zeros((step - wide, chan), jnp.float32)
        grad = wide_ref[...].astype(jnp.bfloat16)
        grad_refs[n][...] = grad
        beside = jnp.concatenate(columns_beside(x_refs[n], flat, spread, m, high), axis=1)
        beside_ref[n * (rows + 2 * step) : (n + 1) * (rows + 2 * step), :] = beside
        lines = []
        for a in range(3):
            pieces = [jnp.zeros((a * step, chan), jnp.bfloat16)] if a else []
            pieces.append(grad)
            pieces += [jnp.zeros(((2 - a) * step, chan), jnp.bfloat16)] if a < 2 else []
            lines.append(jnp.concatenate(pieces, axis=0))
        right.append(jnp.concatenate(lines, axis=1))
    total = lax.dot_general(
        beside_ref[...],
        jnp.concatenate(right, axis=0),
        (((0,), (0,)), ((), ())),
        preferred_element_type=jnp.float32,
    )
    for a, p in enumerate(parts):
        move = total[:, a * chan : (a + 1) * chan] * (step_size * scale / LOSS_SCALE)
        new_v = MOMENTUM * v_ref[p, :] - move
        old = w_ref[p, :]
        if merge:
            old = 0.5 * (old + peer_ref[p, :].astype(jnp.float32))
        half = old + MOMENTUM * new_v - move
        sent[p, :] = half.astype(jnp.bfloat16)
        half_ref[p, :] = half
        new_v_ref[p, :] = new_v


def input_gradient_kernel(blocks, m, scale, stores, *refs):
    grad_refs, kernel_ref, refs = refs[:blocks], refs[blocks], refs[blocks + 1 :]
    if stores:
        v_ref, *out_refs, v_hbm, sem = refs
        store = pltpu.make_async_copy(v_ref, v_hbm, sem)
        store.start()
    else:
        out_refs = refs
    rows, chan = grad_refs[0].shape
    step = LINE * m
    depth = kernel_ref.shape[0] // 3
    share = depth // 3
    edge = jnp.zeros((step, chan), jnp.bfloat16)
    for n in range(blocks):
        grad = jnp.concatenate([edge, grad_refs[n][...], edge], axis=0)
        total = None
        for a in range(3):
            term = lax.dot_general(
                grad[(2 - a) * step : (2 - a) * step + rows],
                kernel_ref[a * depth : (a + 1) * depth, :],
                (((1,), (1,)), ((), ())),
                preferred_element_type=jnp.float32,
            )
            total = term if total is None else total + term
        out = total[:, share : 2 * share]
        out += pltpu.roll(total[:, :share], rows - m, 0)
        out += pltpu.roll(total[:, 2 * share :], m, 0)
        out_refs[n][...] = (out * scale).astype(jnp.bfloat16)
    if stores:
        store.wait()


def split_kernel(turn, share, maps, mine, theirs, sems):
    me = lax.axis_index("group")
    copies = []
    for k, (dst, spot) in enumerate([(theirs, 1 - me), (mine, me)]):
        channels = pl.ds(pl.multiple_of(spot * share, share), share)
        copies.append(pltpu.make_async_copy(maps.at[turn, :, :, :, channels], dst, sems.at[k]))
        copies[-1].start()
    for copy in copies:
        copy.wait()


def finish_kernel(pair, high, wide, share, *refs):
    half_ref, peer_ref, *refs = refs
    if pair:
        *blocks, w_hbm, grads_hbm, w, sems, out_sems = refs
        stores = []
        spots = [lax.axis_index("group"), 1 - lax.axis_index("group")]
        for k, block in enumerate(blocks):
            channels = pl.ds(pl.multiple_of(spots[k % 2] * share, share), share)
            src = block.at[pl.ds(0, high), pl.ds(0, wide)]
            stores.append(pltpu.make_async_copy(src, grads_hbm.at[k // 2, :, :, :, channels], sems.at[k]))
            stores[-1].start()
    else:
        (w_hbm, w, out_sems), stores = refs, []
    depth = w.shape[0] // 3
    for a in range(3):
        p = pl.ds(a * depth, depth)
        w[p, :] = 0.5 * (half_ref[p, :] + peer_ref[p, :].astype(jnp.float32))
        stores.append(pltpu.make_async_copy(w.at[p], w_hbm.at[p], out_sems.at[a]))
        stores[-1].start()
    for copy in stores:
        copy.wait()


PARAMS = pltpu.CompilerParams(vmem_limit_bytes=24 * 1024 * 1024)
VMEM = pl.BlockSpec(memory_space=pltpu.VMEM)
HBM = pl.BlockSpec(memory_space=pltpu.HBM)
SMEM = pl.BlockSpec(memory_space=pltpu.SMEM)
DMA = pltpu.SemaphoreType.DMA


def f32(*shape, space=jax.ShapeDtypeStruct):
    return space(shape, jnp.float32)


def b16(*shape, space=jax.ShapeDtypeStruct):
    return space(shape, jnp.bfloat16)


def conv_scale(chan):
    return 1.0 / math.sqrt(9 * chan)


def forward(xs, weights, m, high):
    blocks = len(xs)
    depth, chan = weights[0].shape
    positions, share = xs[0].shape
    merge = len(weights) == 2
    return pl.pallas_call(
        partial(forward_kernel, blocks, m, high, merge),
        out_shape=[f32(positions, chan)] * blocks + [b16(blocks, positions, chan)] + [b16(depth, chan)] * merge,
        scratch_shapes=[
            pltpu.VMEM((positions, share), jnp.float32),
            pltpu.VMEM(((high + 2) * LINE * m, share), jnp.float32),
        ],
        compiler_params=PARAMS,
        cost_estimate=pl.CostEstimate(
            flops=2 * blocks * positions * depth * chan, bytes_accessed=4 * depth * chan, transcendentals=0
        ),
        name="forward",
    )(*xs, *weights)


def backward(xs, own, other, labels, head, weights, v, m, high, classes):
    blocks = len(own)
    depth, chan = v.shape
    positions, share = xs[0].shape
    rows = high * LINE * m
    scale = conv_scale(chan)
    step_size = 0.1 * 9 * chan
    merge = len(weights) == 2
    scratch = [
        pltpu.VMEM((positions, share), jnp.float32),
        pltpu.VMEM((rows + 2 * LINE * m, share), jnp.float32),
        pltpu.VMEM((blocks * (rows + 2 * LINE * m), 3 * share), jnp.bfloat16),
        pltpu.VMEM((blocks, positions, chan), jnp.float32),
        pltpu.VMEM((rows, chan), jnp.float32),
    ]
    place = {"space": pltpu.VMEM} if blocks == 2 else {}
    return pl.pallas_call(
        partial(backward_kernel, blocks, len(other), m, high, classes, scale, step_size, merge),
        in_specs=[VMEM] * (2 * blocks + len(other)) + [SMEM] + [VMEM] * (2 + len(weights)),
        out_shape=[b16(depth, chan)] + [f32(depth, chan, **place)] * 2 + [b16(rows, chan, **place)] * blocks,
        out_specs=[VMEM] * (3 + blocks),
        scratch_shapes=scratch,
        compiler_params=PARAMS,
        cost_estimate=pl.CostEstimate(
            flops=2 * blocks * rows * v.size, bytes_accessed=20 * v.size, transcendentals=blocks * rows * chan
        ),
        name="backward",
    )(*xs, *own, *other, labels, head, weights[0], v, *weights[1:])


def input_gradient(grads, kernel, m, v=()):
    blocks = len(grads)
    rows, chan = grads[0].shape
    share = kernel.shape[0] // 9
    stores = len(v)
    return pl.pallas_call(
        partial(input_gradient_kernel, blocks, m, conv_scale(chan), stores),
        in_specs=[VMEM] * (blocks + 1) + [pl.BlockSpec(memory_space=pl.ANY)] * stores,
        out_shape=[b16(rows, share)] * blocks + [f32(*x.shape, space=pltpu.HBM) for x in v],
        out_specs=[VMEM] * blocks + [HBM] * stores,
        scratch_shapes=[DMA] * stores,
        compiler_params=PARAMS,
        cost_estimate=pl.CostEstimate(flops=1, bytes_accessed=1, transcendentals=0),
        name="input_gradient",
    )(*grads, kernel, *v)


def split(maps, turn):
    _, high, wide, m, chan = maps.shape
    share = chan // 2
    mine, theirs = pl.pallas_call(
        partial(split_kernel, turn, share),
        in_specs=[pl.BlockSpec(memory_space=pl.ANY)],
        out_shape=[b16(high, wide, m, share)] * 2,
        out_specs=[pl.BlockSpec(memory_space=pl.ANY)] * 2,
        scratch_shapes=[DMA((2,))],
        compiler_params=PARAMS,
        cost_estimate=pl.CostEstimate(flops=1, bytes_accessed=1, transcendentals=0),
        name="split",
    )(maps)
    return mine.reshape(-1, share), theirs.reshape(-1, share)


def finish(half, peer, blocks, high, wide, m):
    depth, chan = half.shape
    share = depth // 9
    pair = len(blocks) > 0
    blocks = [block.reshape(high, LINE, m, share) for block in blocks]
    grads = [b16(ITERS, high, wide, m, chan, space=pltpu.HBM)] if pair else []
    outs = pl.pallas_call(
        partial(finish_kernel, pair, high, wide, share),
        in_specs=[VMEM] * 2 + [pl.BlockSpec(memory_space=pl.ANY)] * len(blocks),
        out_shape=[f32(depth, chan, space=pltpu.HBM)] + grads,
        out_specs=[HBM] * (1 + pair),
        scratch_shapes=[pltpu.VMEM((depth, chan), jnp.float32)] + [DMA((2 * ITERS,))] * pair + [DMA((3,))],
        compiler_params=PARAMS,
        cost_estimate=pl.CostEstimate(flops=1, bytes_accessed=1, transcendentals=0),
        name="finish",
    )(half, peer, *blocks)
    return outs if pair else (outs[0], None)


def run(position, images, labels, weights, velocity, head_weight):
    shape = weights.shape
    maps = jnp.transpose(images[:, 0], (0, 2, 3, 1, 4))
    labels = labels[:, 0]
    _, high, wide, m, chan = maps.shape
    share = shape[3]
    members = lax.axis_size("group")
    bits = lax.axis_size("replica").bit_length() - 1
    classes = head_weight.shape[0]
    pair = members == 2
    w = weights.reshape(9 * share, chan)
    v = velocity.reshape(9 * share, chan)
    head = jnp.pad(head_weight, ((0, -classes % 128), (0, 0)))

    def flat(part):
        return part.reshape(high * wide * m, share)

    def send_back(parts):
        parts = [part.reshape(high, LINE, m, share)[:, :wide] for part in parts]
        parts = lax.all_to_all(jnp.stack(parts), "group", split_axis=0, concat_axis=0, tiled=True)
        return jnp.concatenate([parts[k] for k in range(members)], axis=3)

    if pair:
        mine, theirs = split(maps, 0)
        came = shifted(theirs, "group", 1)
        xs = [mine, came]
    else:
        shares = maps.reshape(ITERS, high, wide, m, members, share)
        shares = lax.all_to_all(shares, "group", split_axis=4, concat_axis=4, tiled=True)
        labels = lax.all_gather(labels, "group", axis=1, tiled=True)
        xs, later = [[flat(shares[t, :, :, :, k]) for k in range(members)] for t in range(ITERS)]

    def add_up(own, sent):
        if pair:
            return own, [shifted(sent, "group", 1)]
        return [lax.psum(part, "group") for part in own], []

    kernel = w.astype(jnp.bfloat16)
    if pair:
        own_a, sent_a = forward([mine], [kernel], m, high)
        other_b = shifted(sent_a, "group", 1)
        own_b, sent_b = forward([came], [kernel], m, high)
        other_a = shifted(sent_b, "group", 1)
        labels, sent_b = lax.optimization_barrier((labels, sent_b))
        labels = jnp.concatenate([labels, shifted(labels, "group", 1)], axis=1)
        own, other = [own_a, own_b], [other_a, other_b]
    else:
        *own, sent = forward(xs, [kernel], m, high)
        own, other = add_up(own, sent)
    sent, half, v, *grads = backward(xs, own, other, labels[:1], head, [w], v, m, high, classes)

    def rest(distance, second, half, sent, v, grads, w, labels, head):
        peer = shifted(sent, "replica", distance)
        if pair:
            mine, theirs = split(maps, 1)
            xs = [mine, shifted(theirs, "group", 1)]
        else:
            xs = later
        *own, sent, kernel = forward(xs, [half, peer], m, high)
        own, other = add_up(own, sent)
        grads, w, sent = lax.optimization_barrier((grads, w, sent))
        parts = input_gradient(grads, w.astype(jnp.bfloat16), m)
        sent, half, v, *grads = backward(xs, own, other, labels[1:], head, [half, peer], v, m, high, classes)
        if pair:
            parts, sent = lax.optimization_barrier((parts, sent))
        peer = shifted(sent, "replica", second)
        *last, v = input_gradient(grads, kernel, m, [v])
        if pair:
            blocks = [parts[0], shifted(parts[1], "group", 1), last[0], shifted(last[1], "group", 1)]
            w, grads_in = finish(half, peer, blocks, high, wide, m)
        else:
            w, _ = finish(half, peer, [], high, wide, m)
            grads_in = jnp.stack([send_back(parts), send_back(last)])
        return w, v, grads_in

    w, v, grads_in = rest(1 << position, 1 << (position + 1) % bits, half, sent, v, grads, w, labels, head)
    grads_in = jnp.transpose(grads_in, (0, 3, 1, 2, 4))[:, None]
    return (w.reshape(shape), v.reshape(shape), grads_in)


def local(images, labels, step_index, weights, velocity, head_weight):
    bits = lax.axis_size("replica").bit_length() - 1
    branches = [partial(run, position) for position in range(bits)]
    return lax.switch(step_index[0] % bits, branches, images, labels, weights, velocity, head_weight)


def solution(mesh):
    return jax.shard_map(
        local,
        mesh=mesh,
        in_specs=(
            P(None, "replica", "group", None, None, None),
            P(None, "replica", "group"),
            P(),
            P("replica", None, None, "group", None),
            P("replica", None, None, "group", None),
            P(),
        ),
        out_specs=(
            P("replica", None, None, "group", None),
            P("replica", None, None, "group", None),
            P(None, "replica", "group", None, None, None),
        ),
        check_vma=False,
    )
```

```python
from functools import partial
import math

import jax
import jax.numpy as jnp
from jax import lax
from jax.experimental import pallas as pl
from jax.experimental.pallas import tpu as pltpu
from jax.sharding import PartitionSpec as P

ITERS = 2

MOMENTUM = 0.9
LOSS_SCALE = 256.0
LINE = 16
SUB = 8
CHUNKS = 2


def shifted(x, axis, by):
    length = lax.axis_size(axis)
    return lax.ppermute(x, axis, [(i, (i + by) % length) for i in range(length)])


def line_by_line(dst, src, lines, wide, to, at, start=0):
    for i in range(lines):
        dst[start + i * to : start + i * to + wide, :] = src[i * at : i * at + wide, :]


def columns_beside(x_ref, flat, spread, m, high):
    wide, step = x_ref.shape[0] // high, LINE * m
    flat[...] = x_ref[...].astype(jnp.float32)
    spread[...] = jnp.zeros_like(spread)
    line_by_line(spread, flat, high, wide, step, wide, step)
    rows = spread[...]
    beside = [pltpu.roll(rows, m, 0), rows, pltpu.roll(rows, rows.shape[0] - m, 0)]
    return [part.astype(jnp.bfloat16) for part in beside]


def forward_kernel(blocks, m, high, merge, chunk, cast, noted, *refs):
    refs = list(refs)
    x_refs, refs = refs[:blocks], refs[blocks:]
    if noted:
        note_ref, *refs = refs
    if cast:
        w_ref, *refs, kernel_ref, flat, spread = refs
        kernel_ref[...] = w_ref[...].astype(jnp.bfloat16)
        refs = [kernel_ref, *refs, flat, spread]
    wide, step = x_refs[0].shape[0] // high, LINE * m
    rows = high * step
    if merge:
        half_ref, peer_ref, *pre_refs, sent_ref, kernel_ref, flat, spread = refs
        count = peer_ref.shape[1]
        half = half_ref[:, chunk * count : (chunk + 1) * count]
        kernel_ref[...] = (0.5 * (half + peer_ref[...].astype(jnp.float32))).astype(jnp.bfloat16)
    else:
        kernel_ref, *pre_refs, sent_ref, flat, spread = refs
    for n in range(blocks):
        beside = columns_beside(x_refs[n], flat, spread, m, high)
        lines = [part[a * step : a * step + rows] for a in range(3) for part in beside]
        part = jnp.dot(jnp.concatenate(lines, axis=1), kernel_ref[...], preferred_element_type=jnp.float32)
        for i in range(high):
            pre_refs[n][i * wide : (i + 1) * wide, :] = part[i * step : i * step + wide]
        spot = (n + 1) % blocks if blocks == 2 else n
        if noted:
            sent_ref[spot, : high * wide, :] = pre_refs[n][...].astype(jnp.bfloat16)
        else:
            sent_ref[spot] = pre_refs[n][...].astype(jnp.bfloat16)
    if noted:
        sent_ref[0, high * wide :, :] = note_ref[...]


def beside_each_other(refs):
    return jnp.concatenate([ref[...] for ref in refs], axis=1) if len(refs) > 1 else refs[0][...]


def backward_kernel(blocks, chunks, by_block, notes, now, peers, sends, m, high, classes, scale, step_size, *refs):
    refs = list(refs)

    def take(count):
        return [refs.pop(0) for _ in range(count)]

    x_refs = take(blocks)
    own_refs = [take(blocks) for _ in range(chunks)]
    other_refs = take({True: blocks, False: chunks, None: 0}[by_block])
    note_refs = take(notes)
    label_refs = take(0 if notes else 1)
    head, w_ref, v_ref = take(3)
    peer_refs, sent_refs = take(peers), take(sends)
    half_ref, new_v_ref = take(2)
    grad_refs = take(blocks)
    flat, spread, beside_ref, slope_ref, wide_ref = refs
    wide, step = x_refs[0].shape[0] // high, LINE * m
    rows = high * step
    area = wide // m * high
    depth, chan = w_ref.shape[0] // 3, w_ref.shape[1]
    parts = [pl.ds(a * depth, depth) for a in range(3)]
    turn = lax.broadcasted_iota(jnp.int32, (SUB, chan), 0) % m
    pooled = []
    for n in range(blocks):
        pre = beside_each_other([own_refs[c][n] for c in range(chunks)])
        if by_block is not None:
            other = other_refs[n][0, : flat.shape[0], :] if by_block else jnp.concatenate([ref[n] for ref in other_refs], axis=1)
            pre = pre + other.astype(jnp.float32)
        pre = pre * scale
        sig = jax.nn.sigmoid(pre)
        slope_ref[n] = sig * (1.0 + pre * (1.0 - sig))
        total = jnp.sum((pre * sig).reshape(-1, SUB, chan), axis=0)
        pooled += [jnp.sum(jnp.where(turn == k, total, 0.0), axis=0, keepdims=True) for k in range(m)]
    pooled = (jnp.concatenate(pooled, axis=0) / area).astype(jnp.bfloat16)
    logits = lax.dot_general(pooled, head[...], (((1,), (1,)), ((), ())), preferred_element_type=jnp.float32)
    klass = lax.broadcasted_iota(jnp.int32, logits.shape, 1)
    image = lax.broadcasted_iota(jnp.int32, logits.shape, 0)
    logits = jnp.where(klass < classes, logits, -jnp.inf)
    expo = jnp.exp(logits - jnp.max(logits, axis=1, keepdims=True))
    probs = expo / jnp.sum(expo, axis=1, keepdims=True)
    target = jnp.zeros(logits.shape, jnp.int32)
    for ref in label_refs:
        for n in range(ref.shape[1] * ref.shape[2]):
            target = jnp.where(image == n, ref[now, n // ref.shape[2], n % ref.shape[2]], target)
    if notes:
        for k, note in enumerate([note_refs[0][...], note_refs[1][0, flat.shape[0] :, :]]):
            digits = note.astype(jnp.float32).astype(jnp.int32)
            label = digits[:, : chan // 2] * 32 + digits[:, chan // 2 :]
            label = jnp.concatenate([label] * (head.shape[0] // (chan // 2)), axis=1)
            for n in range(m):
                target = jnp.where(image == k * m + n, label[now * m + n : now * m + n + 1], target)
    onehot = (target == klass).astype(jnp.float32)
    dlogits = (LOSS_SCALE * (probs - onehot)).astype(jnp.bfloat16)
    dpooled = jnp.dot(dlogits, head[...], preferred_element_type=jnp.float32) / area
    right = []
    for n in range(blocks):
        tile = jnp.zeros((SUB, chan), jnp.float32)
        for k in range(m):
            tile = jnp.where(turn == k, dpooled[n * m + k : n * m + k + 1], tile)
        slope_ref[n] = (slope_ref[n].reshape(-1, SUB, chan) * tile[None]).reshape(-1, chan)
        for i in range(high):
            wide_ref[i * step : i * step + wide, :] = slope_ref[n, i * wide : (i + 1) * wide, :]
            wide_ref[i * step + wide : (i + 1) * step, :] = jnp.zeros((step - wide, chan), jnp.float32)
        grad = wide_ref[...].astype(jnp.bfloat16)
        grad_refs[n][...] = grad
        beside = jnp.concatenate(columns_beside(x_refs[n], flat, spread, m, high), axis=1)
        beside_ref[n * (rows + 2 * step) : (n + 1) * (rows + 2 * step), :] = beside
        lines = []
        for a in range(3):
            pieces = [jnp.zeros((a * step, chan), jnp.bfloat16)] if a else []
            pieces.append(grad)
            pieces += [jnp.zeros(((2 - a) * step, chan), jnp.bfloat16)] if a < 2 else []
            lines.append(jnp.concatenate(pieces, axis=0))
        right.append(jnp.concatenate(lines, axis=1))
    total = lax.dot_general(
        beside_ref[...],
        jnp.concatenate(right, axis=0),
        (((0,), (0,)), ((), ())),
        preferred_element_type=jnp.float32,
    )
    for a, p in enumerate(parts):
        move = total[:, a * chan : (a + 1) * chan] * (step_size * scale / LOSS_SCALE)
        new_v = MOMENTUM * v_ref[p, :] - move
        old = w_ref[p, :]
        if peers:
            old = 0.5 * (old + beside_each_other([ref.at[p] for ref in peer_refs]).astype(jnp.float32))
        half = old + MOMENTUM * new_v - move
        for c, ref in enumerate(sent_refs):
            ref[p, :] = half[:, c * (chan // sends) : (c + 1) * (chan // sends)].astype(jnp.bfloat16)
        half_ref[p, :] = half
        new_v_ref[p, :] = new_v


def input_gradient_kernel(blocks, chunks, m, scale, stores, *refs):
    grad_refs, kernel_refs, refs = refs[:blocks], refs[blocks : blocks + chunks], refs[blocks + chunks :]
    if stores:
        v_ref, *out_refs, v_hbm, sem = refs
        store = pltpu.make_async_copy(v_ref, v_hbm, sem)
        store.start()
    else:
        out_refs = refs
    rows, chan = grad_refs[0].shape
    step = LINE * m
    depth = kernel_refs[0].shape[0] // 3
    share = depth // 3
    edge = jnp.zeros((step, chan), jnp.bfloat16)
    for n in range(blocks):
        grad = jnp.concatenate([edge, grad_refs[n][...], edge], axis=0)
        total = None
        for a in range(3):
            term = lax.dot_general(
                grad[(2 - a) * step : (2 - a) * step + rows],
                beside_each_other([ref.at[a * depth : (a + 1) * depth] for ref in kernel_refs]),
                (((1,), (1,)), ((), ())),
                preferred_element_type=jnp.float32,
            )
            total = term if total is None else total + term
        out = total[:, share : 2 * share]
        out += pltpu.roll(total[:, :share], rows - m, 0)
        out += pltpu.roll(total[:, 2 * share :], m, 0)
        out_refs[n][...] = (out * scale).astype(jnp.bfloat16)
    if stores:
        store.wait()


def split_kernel(turn, share, casts, *refs):
    if casts:
        maps, w_hbm, labels_hbm, mine, theirs, kernel, note, sems, w, w_sems, labels, label_sem = refs
        fetch_labels = pltpu.make_async_copy(labels_hbm, labels, label_sem)
        fetch_labels.start()
        depth = w.shape[0] // w_sems.shape[0]
        parts = [pl.ds(a * depth, depth) for a in range(w_sems.shape[0])]
        fetches = [pltpu.make_async_copy(w_hbm.at[p], w.at[p], w_sems.at[a]) for a, p in enumerate(parts)]
        for copy in fetches:
            copy.start()
    else:
        maps, mine, theirs, sems = refs
    me = lax.axis_index("group")
    copies = []
    for k, (dst, spot) in enumerate([(theirs, 1 - me), (mine, me)]):
        channels = pl.ds(pl.multiple_of(spot * share, share), share)
        copies.append(pltpu.make_async_copy(maps.at[turn, :, :, :, channels], dst, sems.at[k]))
        copies[-1].start()
    if casts:
        for copy, p in zip(fetches, parts):
            copy.wait()
            kernel[p, :] = w[p, :].astype(jnp.bfloat16)
        fetch_labels.wait()
        row, lane = [lax.broadcasted_iota(jnp.int32, note.shape, axis) for axis in range(2)]
        digits = jnp.zeros(note.shape, jnp.int32)
        turns, _, m = labels.shape
        for k in range(turns * m):
            label = labels[k // m, 0, k % m]
            digits = jnp.where(row == k, jnp.where(lane < note.shape[1] // 2, label >> 5, label & 31), digits)
        note[...] = digits.astype(jnp.float32).astype(jnp.bfloat16)
    for copy in copies:
        copy.wait()


def finish_kernel(pair, high, wide, share, *refs):
    half_ref, peer_ref, *refs = refs
    if pair:
        *blocks, w_hbm, grads_hbm, w, sems, out_sems = refs
        stores = []
        spots = [lax.axis_index("group"), 1 - lax.axis_index("group")]
        for k, block in enumerate(blocks):
            channels = pl.ds(pl.multiple_of(spots[k % 2] * share, share), share)
            src = block.at[pl.ds(0, high), pl.ds(0, wide)]
            stores.append(pltpu.make_async_copy(src, grads_hbm.at[k // 2, :, :, :, channels], sems.at[k]))
            stores[-1].start()
    else:
        (w_hbm, w, out_sems), stores = refs, []
    depth = w.shape[0] // 3
    for a in range(3):
        p = pl.ds(a * depth, depth)
        w[p, :] = 0.5 * (half_ref[p, :] + peer_ref[p, :].astype(jnp.float32))
        stores.append(pltpu.make_async_copy(w.at[p], w_hbm.at[p], out_sems.at[a]))
        stores[-1].start()
    for copy in stores:
        copy.wait()


PARAMS = pltpu.CompilerParams(vmem_limit_bytes=24 * 1024 * 1024)
VMEM = pl.BlockSpec(memory_space=pltpu.VMEM)
HBM = pl.BlockSpec(memory_space=pltpu.HBM)
SMEM = pl.BlockSpec(memory_space=pltpu.SMEM)
DMA = pltpu.SemaphoreType.DMA


def f32(*shape, space=jax.ShapeDtypeStruct):
    return space(shape, jnp.float32)


def b16(*shape, space=jax.ShapeDtypeStruct):
    return space(shape, jnp.bfloat16)


def conv_scale(chan):
    return 1.0 / math.sqrt(9 * chan)


def forward(xs, weights, m, high, chunk=0, cast=False, notes=()):
    blocks = len(xs)
    depth, chan = weights[-1].shape
    positions, share = xs[0].shape
    merge = len(weights) == 2
    noted = notes[0].shape[0] if notes else 0
    return pl.pallas_call(
        partial(forward_kernel, blocks, m, high, merge, chunk, cast, len(notes)),
        in_specs=[VMEM] * blocks + [VMEM] * (len(notes) + len(weights)),
        out_shape=[f32(positions, chan)] * blocks
        + [b16(blocks, positions + noted, chan)]
        + [b16(depth, chan)] * (merge or cast),
        scratch_shapes=[
            pltpu.VMEM((positions, share), jnp.float32),
            pltpu.VMEM(((high + 2) * LINE * m, share), jnp.float32),
        ],
        compiler_params=PARAMS,
        cost_estimate=pl.CostEstimate(
            flops=2 * blocks * positions * depth * chan, bytes_accessed=4 * depth * chan, transcendentals=0
        ),
        name="forward",
    )(*xs, *notes, *weights)


def backward(xs, own, other, labels, notes, now, head, w, v, peers, sends, m, high, classes):
    blocks, chunks = len(xs), len(own)
    depth, chan = v.shape
    positions, share = xs[0].shape
    rows = high * LINE * m
    scale = conv_scale(chan)
    step_size = 0.1 * 9 * chan
    by_block = None if len(other) == 0 else other[0].shape[0] == 1
    space = pltpu.VMEM if blocks == 2 else jax.ShapeDtypeStruct
    return pl.pallas_call(
        partial(
            backward_kernel,
            blocks,
            chunks,
            by_block,
            len(notes),
            now,
            len(peers),
            sends,
            m,
            high,
            classes,
            scale,
            step_size,
        ),
        in_specs=[VMEM] * (blocks + blocks * chunks + len(other)) + ([VMEM] * len(notes) or [SMEM]) + [VMEM] * (3 + len(peers)),
        out_shape=[b16(depth, chan // sends)] * sends
        + [f32(depth, chan, space=space)] * 2
        + [b16(rows, chan, space=space)] * blocks,
        out_specs=[VMEM] * (sends + 2 + blocks),
        scratch_shapes=[
            pltpu.VMEM((positions, share), jnp.float32),
            pltpu.VMEM((rows + 2 * LINE * m, share), jnp.float32),
            pltpu.VMEM((blocks * (rows + 2 * LINE * m), 3 * share), jnp.bfloat16),
            pltpu.VMEM((blocks, positions, chan), jnp.float32),
            pltpu.VMEM((rows, chan), jnp.float32),
        ],
        compiler_params=PARAMS,
        cost_estimate=pl.CostEstimate(
            flops=2 * blocks * rows * v.size, bytes_accessed=20 * v.size, transcendentals=blocks * rows * chan
        ),
        name="backward",
    )(*xs, *sum(own, []), *other, *(notes or [labels]), head, w, v, *peers)


def input_gradient(grads, kernel, m, v=()):
    blocks = len(grads)
    rows, chan = grads[0].shape
    share = kernel[0].shape[0] // 9
    stores = len(v)
    return pl.pallas_call(
        partial(input_gradient_kernel, blocks, len(kernel), m, conv_scale(chan), stores),
        in_specs=[VMEM] * (blocks + len(kernel)) + [pl.BlockSpec(memory_space=pl.ANY)] * stores,
        out_shape=[b16(rows, share)] * blocks + [f32(*x.shape, space=pltpu.HBM) for x in v],
        out_specs=[VMEM] * blocks + [HBM] * stores,
        scratch_shapes=[DMA] * stores,
        compiler_params=PARAMS,
        cost_estimate=pl.CostEstimate(flops=1, bytes_accessed=1, transcendentals=0),
        name="input_gradient",
    )(*grads, *kernel, *v)


def split(maps, turn, w=None, labels=None):
    _, high, wide, m, chan = maps.shape
    share = chan // 2
    arrays, outs, scratch = [maps], [b16(high, wide, m, share)] * 2, [DMA((2,))]
    casts = w is not None
    if casts:
        arrays += [w, labels]
        rows = labels.size + -(high * wide * m + labels.size) % 16
        outs += [b16(*w.shape, space=pltpu.VMEM), b16(rows, chan, space=pltpu.VMEM)]
        scratch += [pltpu.VMEM(w.shape, jnp.float32), DMA((6,)), pltpu.SMEM(labels.shape, jnp.int32), DMA]
    mine, theirs, *more = pl.pallas_call(
        partial(split_kernel, turn, share, casts),
        in_specs=[pl.BlockSpec(memory_space=pl.ANY)] * len(arrays),
        out_shape=outs,
        out_specs=[pl.BlockSpec(memory_space=pl.ANY)] * 2 + [VMEM] * len(outs[2:]),
        scratch_shapes=scratch,
        compiler_params=PARAMS,
        cost_estimate=pl.CostEstimate(flops=1, bytes_accessed=1, transcendentals=0),
        name="split",
    )(*arrays)
    return mine.reshape(-1, share), theirs.reshape(-1, share), *more


def finish(half, peer, blocks, high, wide, m):
    depth, chan = half.shape
    share = depth // 9
    pair = len(blocks) > 0
    blocks = [block.reshape(high, LINE, m, share) for block in blocks]
    grads = [b16(ITERS, high, wide, m, chan, space=pltpu.HBM)] if pair else []
    outs = pl.pallas_call(
        partial(finish_kernel, pair, high, wide, share),
        in_specs=[VMEM] * 2 + [pl.BlockSpec(memory_space=pl.ANY)] * len(blocks),
        out_shape=[f32(depth, chan, space=pltpu.HBM)] + grads,
        out_specs=[HBM] * (1 + pair),
        scratch_shapes=[pltpu.VMEM((depth, chan), jnp.float32)] + [DMA((2 * ITERS,))] * pair + [DMA((3,))],
        compiler_params=PARAMS,
        cost_estimate=pl.CostEstimate(flops=1, bytes_accessed=1, transcendentals=0),
        name="finish",
    )(half, peer, *blocks)
    return outs if pair else (outs[0], None)


def run(position, images, labels, weights, velocity, head_weight):
    shape = weights.shape
    maps = jnp.transpose(images[:, 0], (0, 2, 3, 1, 4))
    _, high, wide, m, chan = maps.shape
    share = shape[3]
    members = lax.axis_size("group")
    bits = lax.axis_size("replica").bit_length() - 1
    classes = head_weight.shape[0]
    pair = members == 2
    w = weights.reshape(9 * share, chan)
    v = velocity.reshape(9 * share, chan)
    head = jnp.pad(head_weight, ((0, -classes % 128), (0, 0)))

    def flat(part):
        return part.reshape(high * wide * m, share)

    def send_back(parts):
        parts = [part.reshape(high, LINE, m, share)[:, :wide] for part in parts]
        parts = lax.all_to_all(jnp.stack(parts), "group", split_axis=0, concat_axis=0, tiled=True)
        return jnp.concatenate([parts[k] for k in range(members)], axis=3)

    if pair:
        mine, theirs, kernel, note = split(maps, 0, w, labels)
        came = shifted(theirs, "group", 1)
        xs = [mine, came]
    else:
        shares = maps.reshape(ITERS, high, wide, m, members, share)
        shares = lax.all_to_all(shares, "group", split_axis=4, concat_axis=4, tiled=True)
        labels = lax.all_gather(labels, "group", axis=1, tiled=True)
        xs, later = [[flat(shares[t, :, :, :, k]) for k in range(members)] for t in range(ITERS)]

    def add_up(own, sent):
        if pair:
            return own, [shifted(sent, "group", 1)]
        return [lax.psum(part, "group") for part in own], []

    notes = []
    if pair:
        own_a, sent_a = forward([mine], [kernel], m, high, notes=[note])
        other_b = shifted(sent_a, "group", 1)
        own_b, sent_b = forward([came], [kernel], m, high)
        other_a = shifted(sent_b, "group", 1)
        own, other, notes = [own_a, own_b], [other_a, other_b], [note, other_b]
    else:
        *own, sent, kernel = forward(xs, [w], m, high, cast=True)
        own, other = add_up(own, sent)
    made = backward(xs, [own], other, labels, notes, 0, head, w, v, [], CHUNKS, m, high, classes)
    sent, (half, v), grads = made[:CHUNKS], made[CHUNKS : CHUNKS + 2], made[CHUNKS + 2 :]
    old_kernel = [kernel]
    peers = [shifted(part, "replica", 1 << position) for part in sent]
    if pair:
        mine, theirs = split(maps, 1)
        xs = [mine, shifted(theirs, "group", 1)]
    else:
        xs = later
    own, other, kernel = [], [], []
    for chunk, peer in enumerate(peers):
        *parts, sent, part = forward(xs, [half, peer], m, high, chunk)
        parts, came = add_up(parts, sent)
        own.append(parts)
        other += came
        kernel.append(part)
    grads, sent = lax.optimization_barrier((grads, sent))
    parts = input_gradient(grads, old_kernel, m)
    sent, half, v, *grads = backward(
        xs, own, other, labels, notes, 1, head, half, v, peers, 1, m, high, classes
    )
    if pair:
        parts, sent = lax.optimization_barrier((parts, sent))
    peer = shifted(sent, "replica", 1 << (position + 1) % bits)
    *last, v = input_gradient(grads, kernel, m, [v])
    if pair:
        blocks = [parts[0], shifted(parts[1], "group", 1), last[0], shifted(last[1], "group", 1)]
        w, grads_in = finish(half, peer, blocks, high, wide, m)
    else:
        w, _ = finish(half, peer, [], high, wide, m)
        grads_in = jnp.stack([send_back(parts), send_back(last)])
    grads_in = jnp.transpose(grads_in, (0, 3, 1, 2, 4))[:, None]
    return (w.reshape(shape), v.reshape(shape), grads_in)


def local(images, labels, step_index, weights, velocity, head_weight):
    bits = lax.axis_size("replica").bit_length() - 1
    branches = [partial(run, position) for position in range(bits)]
    return lax.switch(step_index[0] % bits, branches, images, labels, weights, velocity, head_weight)


def solution(mesh):
    return jax.shard_map(
        local,
        mesh=mesh,
        in_specs=(
            P(None, "replica", "group", None, None, None),
            P(None, "replica", "group"),
            P(),
            P("replica", None, None, "group", None),
            P("replica", None, None, "group", None),
            P(),
        ),
        out_specs=(
            P("replica", None, None, "group", None),
            P("replica", None, None, "group", None),
            P(None, "replica", "group", None, None, None),
        ),
        check_vma=False,
    )
```

```python
from functools import partial
import math

import jax
import jax.numpy as jnp
from jax import lax
from jax.experimental import pallas as pl
from jax.experimental.pallas import tpu as pltpu
from jax.sharding import PartitionSpec as P

ITERS = 2

MOMENTUM = 0.9
LOSS_SCALE = 256.0
LINE = 16
SUB = 8
CHUNKS = 2


def shifted(x, axis, by):
    length = lax.axis_size(axis)
    return lax.ppermute(x, axis, [(i, (i + by) % length) for i in range(length)])


def line_by_line(dst, src, lines, wide, to, at, start=0):
    for i in range(lines):
        dst[start + i * to : start + i * to + wide, :] = src[i * at : i * at + wide, :]


def columns_beside(x_ref, flat, spread, m, high):
    wide, step = x_ref.shape[0] // high, LINE * m
    flat[...] = x_ref[...].astype(jnp.float32)
    spread[...] = jnp.zeros_like(spread)
    line_by_line(spread, flat, high, wide, step, wide, step)
    rows = spread[...]
    beside = [pltpu.roll(rows, m, 0), rows, pltpu.roll(rows, rows.shape[0] - m, 0)]
    return [part.astype(jnp.bfloat16) for part in beside]


def forward_kernel(blocks, m, high, merge, chunk, cast, noted, *refs):
    refs = list(refs)
    x_refs, refs = refs[:blocks], refs[blocks:]
    if noted:
        note_ref, *refs = refs
    if cast:
        w_ref, *refs, kernel_ref, flat, spread = refs
        kernel_ref[...] = w_ref[...].astype(jnp.bfloat16)
        refs = [kernel_ref, *refs, flat, spread]
    wide, step = x_refs[0].shape[0] // high, LINE * m
    rows = high * step
    if merge:
        half_ref, peer_ref, *pre_refs, sent_ref, kernel_ref, flat, spread = refs
        count = peer_ref.shape[1]
        half = half_ref[:, chunk * count : (chunk + 1) * count]
        kernel_ref[...] = (0.5 * (half + peer_ref[...].astype(jnp.float32))).astype(jnp.bfloat16)
    else:
        kernel_ref, *pre_refs, sent_ref, flat, spread = refs
    for n in range(blocks):
        beside = columns_beside(x_refs[n], flat, spread, m, high)
        lines = [part[a * step : a * step + rows] for a in range(3) for part in beside]
        part = jnp.dot(jnp.concatenate(lines, axis=1), kernel_ref[...], preferred_element_type=jnp.float32)
        for i in range(high):
            pre_refs[n][i * wide : (i + 1) * wide, :] = part[i * step : i * step + wide]
        spot = (n + 1) % blocks if blocks == 2 else n
        if noted:
            sent_ref[spot, : high * wide, :] = pre_refs[n][...].astype(jnp.bfloat16)
        else:
            sent_ref[spot] = pre_refs[n][...].astype(jnp.bfloat16)
    if noted:
        sent_ref[0, high * wide :, :] = note_ref[...]


def beside_each_other(refs):
    return jnp.concatenate([ref[...] for ref in refs], axis=1) if len(refs) > 1 else refs[0][...]


def backward_kernel(blocks, chunks, by_block, notes, now, peers, sends, m, high, classes, scale, step_size, *refs):
    refs = list(refs)

    def take(count):
        return [refs.pop(0) for _ in range(count)]

    x_refs = take(blocks)
    own_refs = [take(blocks) for _ in range(chunks)]
    other_refs = take({True: blocks, False: chunks, None: 0}[by_block])
    note_refs = take(notes)
    label_refs = take(0 if notes else 1)
    head, w_ref, v_ref = take(3)
    peer_refs, sent_refs = take(peers), take(sends)
    half_ref, new_v_ref = take(2)
    grad_refs = take(blocks)
    flat, spread, beside_ref, slope_ref, wide_ref = refs
    wide, step = x_refs[0].shape[0] // high, LINE * m
    rows = high * step
    area = wide // m * high
    depth, chan = w_ref.shape[0] // 3, w_ref.shape[1]
    parts = [pl.ds(a * depth, depth) for a in range(3)]
    turn = lax.broadcasted_iota(jnp.int32, (SUB, chan), 0) % m
    pooled = []
    for n in range(blocks):
        pre = beside_each_other([own_refs[c][n] for c in range(chunks)])
        if by_block is not None:
            other = other_refs[n][0, : flat.shape[0], :] if by_block else jnp.concatenate([ref[n] for ref in other_refs], axis=1)
            pre = pre + other.astype(jnp.float32)
        pre = pre * scale
        sig = jax.nn.sigmoid(pre)
        slope_ref[n] = sig * (1.0 + pre * (1.0 - sig))
        total = jnp.sum((pre * sig).reshape(-1, SUB, chan), axis=0)
        pooled += [jnp.sum(jnp.where(turn == k, total, 0.0), axis=0, keepdims=True) for k in range(m)]
    pooled = (jnp.concatenate(pooled, axis=0) / area).astype(jnp.bfloat16)
    logits = lax.dot_general(pooled, head[...], (((1,), (1,)), ((), ())), preferred_element_type=jnp.float32)
    klass = lax.broadcasted_iota(jnp.int32, logits.shape, 1)
    image = lax.broadcasted_iota(jnp.int32, logits.shape, 0)
    logits = jnp.where(klass < classes, logits, -jnp.inf)
    expo = jnp.exp(logits - jnp.max(logits, axis=1, keepdims=True))
    probs = expo / jnp.sum(expo, axis=1, keepdims=True)
    target = jnp.zeros(logits.shape, jnp.int32)
    for ref in label_refs:
        for n in range(ref.shape[1] * ref.shape[2]):
            target = jnp.where(image == n, ref[now, n // ref.shape[2], n % ref.shape[2]], target)
    if notes:
        for k, note in enumerate([note_refs[0][...], note_refs[1][0, flat.shape[0] :, :]]):
            digits = note.astype(jnp.float32).astype(jnp.int32)
            label = digits[:, : chan // 2] * 32 + digits[:, chan // 2 :]
            label = jnp.concatenate([label] * (head.shape[0] // (chan // 2)), axis=1)
            for n in range(m):
                target = jnp.where(image == k * m + n, label[now * m + n : now * m + n + 1], target)
    onehot = (target == klass).astype(jnp.float32)
    dlogits = (LOSS_SCALE * (probs - onehot)).astype(jnp.bfloat16)
    dpooled = jnp.dot(dlogits, head[...], preferred_element_type=jnp.float32) / area
    right = []
    for n in range(blocks):
        tile = jnp.zeros((SUB, chan), jnp.float32)
        for k in range(m):
            tile = jnp.where(turn == k, dpooled[n * m + k : n * m + k + 1], tile)
        slope_ref[n] = (slope_ref[n].reshape(-1, SUB, chan) * tile[None]).reshape(-1, chan)
        for i in range(high):
            wide_ref[i * step : i * step + wide, :] = slope_ref[n, i * wide : (i + 1) * wide, :]
            wide_ref[i * step + wide : (i + 1) * step, :] = jnp.zeros((step - wide, chan), jnp.float32)
        grad = wide_ref[...].astype(jnp.bfloat16)
        grad_refs[n][...] = grad
        beside = jnp.concatenate(columns_beside(x_refs[n], flat, spread, m, high), axis=1)
        beside_ref[n * (rows + 2 * step) : (n + 1) * (rows + 2 * step), :] = beside
        lines = []
        for a in range(3):
            pieces = [jnp.zeros((a * step, chan), jnp.bfloat16)] if a else []
            pieces.append(grad)
            pieces += [jnp.zeros(((2 - a) * step, chan), jnp.bfloat16)] if a < 2 else []
            lines.append(jnp.concatenate(pieces, axis=0))
        right.append(jnp.concatenate(lines, axis=1))
    total = lax.dot_general(
        beside_ref[...],
        jnp.concatenate(right, axis=0),
        (((0,), (0,)), ((), ())),
        preferred_element_type=jnp.float32,
    )
    for a, p in enumerate(parts):
        move = total[:, a * chan : (a + 1) * chan] * (step_size * scale / LOSS_SCALE)
        new_v = MOMENTUM * v_ref[p, :] - move
        old = w_ref[p, :]
        if peers:
            old = 0.5 * (old + beside_each_other([ref.at[p] for ref in peer_refs]).astype(jnp.float32))
        half = old + MOMENTUM * new_v - move
        for c, ref in enumerate(sent_refs):
            ref[p, :] = half[:, c * (chan // sends) : (c + 1) * (chan // sends)].astype(jnp.bfloat16)
        half_ref[p, :] = half
        new_v_ref[p, :] = new_v


def input_gradient_kernel(blocks, chunks, m, scale, stores, *refs):
    grad_refs, kernel_refs, refs = refs[:blocks], refs[blocks : blocks + chunks], refs[blocks + chunks :]
    if stores:
        v_ref, *out_refs, v_hbm, padded, outs, sem = refs
        store = pltpu.make_async_copy(v_ref, v_hbm, sem)
        store.start()
    else:
        *out_refs, padded, outs = refs
    rows, chan = grad_refs[0].shape
    step = LINE * m
    depth = kernel_refs[0].shape[0] // 3
    share = depth // 3
    edge = jnp.zeros((step, chan), jnp.bfloat16)
    for n in range(blocks):
        padded[n, :step, :] = edge
        padded[n, step : step + rows, :] = grad_refs[n][...]
        padded[n, step + rows :, :] = edge

    def block(n, carry):
        total = None
        for a in range(3):
            term = lax.dot_general(
                padded[n, (2 - a) * step : (2 - a) * step + rows, :],
                beside_each_other([ref.at[a * depth : (a + 1) * depth] for ref in kernel_refs]),
                (((1,), (1,)), ((), ())),
                preferred_element_type=jnp.float32,
            )
            total = term if total is None else total + term
        out = total[:, share : 2 * share]
        out += pltpu.roll(total[:, :share], rows - m, 0)
        out += pltpu.roll(total[:, 2 * share :], m, 0)
        outs[n] = (out * scale).astype(jnp.bfloat16)
        return carry

    lax.fori_loop(0, blocks, block, 0)
    for n in range(blocks):
        out_refs[n][...] = outs[n]
    if stores:
        store.wait()


def split_kernel(turn, share, casts, *refs):
    if casts:
        maps, w_hbm, labels_hbm, mine, theirs, kernel, note, sems, w, w_sems, labels, label_sem = refs
        fetch_labels = pltpu.make_async_copy(labels_hbm, labels, label_sem)
        fetch_labels.start()
        depth = w.shape[0] // w_sems.shape[0]
        parts = [pl.ds(a * depth, depth) for a in range(w_sems.shape[0])]
        fetches = [pltpu.make_async_copy(w_hbm.at[p], w.at[p], w_sems.at[a]) for a, p in enumerate(parts)]
        for copy in fetches:
            copy.start()
    else:
        maps, mine, theirs, sems = refs
    me = lax.axis_index("group")
    copies = []
    for k, (dst, spot) in enumerate([(theirs, 1 - me), (mine, me)]):
        channels = pl.ds(pl.multiple_of(spot * share, share), share)
        copies.append(pltpu.make_async_copy(maps.at[turn, :, :, :, channels], dst, sems.at[k]))
        copies[-1].start()
    if casts:
        for copy, p in zip(fetches, parts):
            copy.wait()
            kernel[p, :] = w[p, :].astype(jnp.bfloat16)
        fetch_labels.wait()
        row, lane = [lax.broadcasted_iota(jnp.int32, note.shape, axis) for axis in range(2)]
        digits = jnp.zeros(note.shape, jnp.int32)
        turns, _, m = labels.shape
        for k in range(turns * m):
            label = labels[k // m, 0, k % m]
            digits = jnp.where(row == k, jnp.where(lane < note.shape[1] // 2, label >> 5, label & 31), digits)
        note[...] = digits.astype(jnp.float32).astype(jnp.bfloat16)
    for copy in copies:
        copy.wait()


def finish_kernel(chunk, blocks, high, wide, share, *refs):
    half_ref, peer_ref, *refs = refs
    refs = refs[1:] if chunk else refs
    block_refs, refs = refs[:blocks], refs[blocks:]
    w_hbm, *refs = refs
    stores = []
    if blocks:
        grads_hbm, w, out_sems, sems = refs
        spots = [lax.axis_index("group"), 1 - lax.axis_index("group")]
        for k, block in enumerate(block_refs):
            channels = pl.ds(pl.multiple_of(spots[k % 2] * share, share), share)
            src = block.at[pl.ds(0, high), pl.ds(0, wide)]
            stores.append(pltpu.make_async_copy(src, grads_hbm.at[k // 2, :, :, :, channels], sems.at[k]))
            stores[-1].start()
    else:
        w, out_sems = refs
    depth, width = w.shape[0] // 3, w.shape[1]
    columns = pl.ds(chunk * width, width)
    for a in range(3):
        p = pl.ds(a * depth, depth)
        w[p, :] = 0.5 * (half_ref[p, columns] + peer_ref[p, :].astype(jnp.float32))
        stores.append(pltpu.make_async_copy(w.at[p], w_hbm.at[p, columns], out_sems.at[a]))
        stores[-1].start()
    for copy in stores:
        copy.wait()


PARAMS = pltpu.CompilerParams(vmem_limit_bytes=24 * 1024 * 1024)
VMEM = pl.BlockSpec(memory_space=pltpu.VMEM)
HBM = pl.BlockSpec(memory_space=pltpu.HBM)
SMEM = pl.BlockSpec(memory_space=pltpu.SMEM)
DMA = pltpu.SemaphoreType.DMA


def f32(*shape, space=jax.ShapeDtypeStruct):
    return space(shape, jnp.float32)


def b16(*shape, space=jax.ShapeDtypeStruct):
    return space(shape, jnp.bfloat16)


def conv_scale(chan):
    return 1.0 / math.sqrt(9 * chan)


def forward(xs, weights, m, high, chunk=0, cast=False, notes=()):
    blocks = len(xs)
    depth, chan = weights[-1].shape
    positions, share = xs[0].shape
    merge = len(weights) == 2
    noted = notes[0].shape[0] if notes else 0
    return pl.pallas_call(
        partial(forward_kernel, blocks, m, high, merge, chunk, cast, len(notes)),
        in_specs=[VMEM] * blocks + [VMEM] * (len(notes) + len(weights)),
        out_shape=[f32(positions, chan)] * blocks
        + [b16(blocks, positions + noted, chan)]
        + [b16(depth, chan)] * (merge or cast),
        scratch_shapes=[
            pltpu.VMEM((positions, share), jnp.float32),
            pltpu.VMEM(((high + 2) * LINE * m, share), jnp.float32),
        ],
        compiler_params=PARAMS,
        cost_estimate=pl.CostEstimate(
            flops=2 * blocks * positions * depth * chan, bytes_accessed=4 * depth * chan, transcendentals=0
        ),
        name="forward",
    )(*xs, *notes, *weights)


def backward(xs, own, other, labels, notes, now, head, w, v, peers, sends, m, high, classes):
    blocks, chunks = len(xs), len(own)
    depth, chan = v.shape
    positions, share = xs[0].shape
    rows = high * LINE * m
    scale = conv_scale(chan)
    step_size = 0.1 * 9 * chan
    by_block = None if len(other) == 0 else other[0].shape[0] == 1
    space = pltpu.VMEM if blocks == 2 else jax.ShapeDtypeStruct
    return pl.pallas_call(
        partial(
            backward_kernel,
            blocks,
            chunks,
            by_block,
            len(notes),
            now,
            len(peers),
            sends,
            m,
            high,
            classes,
            scale,
            step_size,
        ),
        in_specs=[VMEM] * (blocks + blocks * chunks + len(other)) + ([VMEM] * len(notes) or [SMEM]) + [VMEM] * (3 + len(peers)),
        out_shape=[b16(depth, chan // sends)] * sends
        + [f32(depth, chan, space=space)] * 2
        + [b16(rows, chan, space=space)] * blocks,
        out_specs=[VMEM] * (sends + 2 + blocks),
        scratch_shapes=[
            pltpu.VMEM((positions, share), jnp.float32),
            pltpu.VMEM((rows + 2 * LINE * m, share), jnp.float32),
            pltpu.VMEM((blocks * (rows + 2 * LINE * m), 3 * share), jnp.bfloat16),
            pltpu.VMEM((blocks, positions, chan), jnp.float32),
            pltpu.VMEM((rows, chan), jnp.float32),
        ],
        compiler_params=PARAMS,
        cost_estimate=pl.CostEstimate(
            flops=2 * blocks * rows * v.size, bytes_accessed=20 * v.size, transcendentals=blocks * rows * chan
        ),
        name="backward",
    )(*xs, *sum(own, []), *other, *(notes or [labels]), head, w, v, *peers)


def input_gradient(grads, kernel, m, v=()):
    blocks = len(grads)
    rows, chan = grads[0].shape
    share = kernel[0].shape[0] // 9
    stores = len(v)
    return pl.pallas_call(
        partial(input_gradient_kernel, blocks, len(kernel), m, conv_scale(chan), stores),
        in_specs=[VMEM] * (blocks + len(kernel)) + [pl.BlockSpec(memory_space=pl.ANY)] * stores,
        out_shape=[b16(rows, share)] * blocks + [f32(*x.shape, space=pltpu.HBM) for x in v],
        out_specs=[VMEM] * blocks + [HBM] * stores,
        scratch_shapes=[
            pltpu.VMEM((blocks, rows + 2 * LINE * m, chan), jnp.bfloat16),
            pltpu.VMEM((blocks, rows, share), jnp.bfloat16),
        ]
        + [DMA] * stores,
        compiler_params=PARAMS,
        cost_estimate=pl.CostEstimate(flops=1, bytes_accessed=1, transcendentals=0),
        name="input_gradient",
    )(*grads, *kernel, *v)


def split(maps, turn, w=None, labels=None):
    _, high, wide, m, chan = maps.shape
    share = chan // 2
    arrays, outs, scratch = [maps], [b16(high, wide, m, share)] * 2, [DMA((2,))]
    casts = w is not None
    if casts:
        arrays += [w, labels]
        rows = labels.size + -(high * wide * m + labels.size) % 16
        outs += [b16(*w.shape, space=pltpu.VMEM), b16(rows, chan, space=pltpu.VMEM)]
        scratch += [pltpu.VMEM(w.shape, jnp.float32), DMA((6,)), pltpu.SMEM(labels.shape, jnp.int32), DMA]
    mine, theirs, *more = pl.pallas_call(
        partial(split_kernel, turn, share, casts),
        in_specs=[pl.BlockSpec(memory_space=pl.ANY)] * len(arrays),
        out_shape=outs,
        out_specs=[pl.BlockSpec(memory_space=pl.ANY)] * 2 + [VMEM] * len(outs[2:]),
        scratch_shapes=scratch,
        compiler_params=PARAMS,
        cost_estimate=pl.CostEstimate(flops=1, bytes_accessed=1, transcendentals=0),
        name="split",
    )(*arrays)
    return mine.reshape(-1, share), theirs.reshape(-1, share), *more


def finish(half, peers, blocks, high, wide, m):
    depth, chan = half.shape
    share = depth // 9
    blocks = [block.reshape(high, LINE, m, share) for block in blocks]
    w, grads = [], []
    for c, peer in enumerate(peers):
        here = blocks if c == 0 else []
        outs = [f32(depth, chan, space=pltpu.HBM)]
        outs += [b16(ITERS, high, wide, m, chan, space=pltpu.HBM)] if here else []
        *w, = pl.pallas_call(
            partial(finish_kernel, c, len(here), high, wide, share),
            in_specs=[VMEM] * 2 + [pl.BlockSpec(memory_space=pl.ANY)] * (len(w) + len(here)),
            out_shape=outs,
            out_specs=[HBM] * len(outs),
            scratch_shapes=[pltpu.VMEM((depth, chan // CHUNKS), jnp.float32), DMA((3,))]
            + [DMA((2 * ITERS,))] * (len(here) > 0),
            input_output_aliases={2: 0} if w else {},
            compiler_params=PARAMS,
            cost_estimate=pl.CostEstimate(flops=1, bytes_accessed=1, transcendentals=0),
            name="finish",
        )(half, peer, *w, *here)
        grads, w = grads or w[1:], w[:1]
    return w[0], grads[0] if grads else None


def run(position, images, labels, weights, velocity, head_weight):
    shape = weights.shape
    maps = jnp.transpose(images[:, 0], (0, 2, 3, 1, 4))
    _, high, wide, m, chan = maps.shape
    share = shape[3]
    members = lax.axis_size("group")
    bits = lax.axis_size("replica").bit_length() - 1
    classes = head_weight.shape[0]
    pair = members == 2
    w = weights.reshape(9 * share, chan)
    v = velocity.reshape(9 * share, chan)
    head = jnp.pad(head_weight, ((0, -classes % 128), (0, 0)))

    def flat(part):
        return part.reshape(high * wide * m, share)

    def send_back(parts):
        parts = [part.reshape(high, LINE, m, share)[:, :wide] for part in parts]
        parts = lax.all_to_all(jnp.stack(parts), "group", split_axis=0, concat_axis=0, tiled=True)
        return jnp.concatenate([parts[k] for k in range(members)], axis=3)

    if pair:
        mine, theirs, kernel, note = split(maps, 0, w, labels)
        came = shifted(theirs, "group", 1)
        xs = [mine, came]
    else:
        shares = maps.reshape(ITERS, high, wide, m, members, share)
        shares = lax.all_to_all(shares, "group", split_axis=4, concat_axis=4, tiled=True)
        labels = lax.all_gather(labels, "group", axis=1, tiled=True)
        xs, later = [[flat(shares[t, :, :, :, k]) for k in range(members)] for t in range(ITERS)]

    def add_up(own, sent):
        if pair:
            return own, [shifted(sent, "group", 1)]
        return [lax.psum(part, "group") for part in own], []

    notes = []
    if pair:
        own_a, sent_a = forward([mine], [kernel], m, high, notes=[note])
        other_b = shifted(sent_a, "group", 1)
        own_b, sent_b = forward([came], [kernel], m, high)
        other_a = shifted(sent_b, "group", 1)
        own, other, notes = [own_a, own_b], [other_a, other_b], [note, other_b]
    else:
        *own, sent, kernel = forward(xs, [w], m, high, cast=True)
        own, other = add_up(own, sent)
    made = backward(xs, [own], other, labels, notes, 0, head, w, v, [], CHUNKS, m, high, classes)
    sent, (half, v), grads = made[:CHUNKS], made[CHUNKS : CHUNKS + 2], made[CHUNKS + 2 :]
    old_kernel = [kernel]
    peers = [shifted(part, "replica", 1 << position) for part in sent]
    if pair:
        mine, theirs = split(maps, 1)
        xs = [mine, shifted(theirs, "group", 1)]
    else:
        xs = later
    own, other, kernel = [], [], []
    for chunk, peer in enumerate(peers):
        *parts, sent, part = forward(xs, [half, peer], m, high, chunk)
        parts, came = add_up(parts, sent)
        own.append(parts)
        other += came
        kernel.append(part)
    grads, sent = lax.optimization_barrier((grads, sent))
    parts = input_gradient(grads, old_kernel, m)
    made = backward(xs, own, other, labels, notes, 1, head, half, v, peers, CHUNKS, m, high, classes)
    sent, (half, v), grads = made[:CHUNKS], made[CHUNKS : CHUNKS + 2], made[CHUNKS + 2 :]
    if pair:
        parts, sent = lax.optimization_barrier((parts, sent))
    peers = [shifted(part, "replica", 1 << (position + 1) % bits) for part in sent]
    *last, v = input_gradient(grads, kernel, m, [v])
    if pair:
        blocks = [parts[0], shifted(parts[1], "group", 1), last[0], shifted(last[1], "group", 1)]
        w, grads_in = finish(half, peers, blocks, high, wide, m)
    else:
        w, _ = finish(half, peers, [], high, wide, m)
        grads_in = jnp.stack([send_back(parts), send_back(last)])
    grads_in = jnp.transpose(grads_in, (0, 3, 1, 2, 4))[:, None]
    return (w.reshape(shape), v.reshape(shape), grads_in)


def local(images, labels, step_index, weights, velocity, head_weight):
    bits = lax.axis_size("replica").bit_length() - 1
    branches = [partial(run, position) for position in range(bits)]
    return lax.switch(step_index[0] % bits, branches, images, labels, weights, velocity, head_weight)


def solution(mesh):
    return jax.shard_map(
        local,
        mesh=mesh,
        in_specs=(
            P(None, "replica", "group", None, None, None),
            P(None, "replica", "group"),
            P(),
            P("replica", None, None, "group", None),
            P("replica", None, None, "group", None),
            P(),
        ),
        out_specs=(
            P("replica", None, None, "group", None),
            P("replica", None, None, "group", None),
            P(None, "replica", "group", None, None, None),
        ),
        check_vma=False,
    )
```

```python
from functools import partial
import math

import jax
import jax.numpy as jnp
from jax import lax
from jax.experimental import pallas as pl
from jax.experimental.pallas import tpu as pltpu
from jax.sharding import PartitionSpec as P

ITERS = 2

MOMENTUM = 0.9
LOSS_SCALE = 256.0
LINE = 16
SUB = 8
CHUNKS = 2


def shifted(x, axis, by):
    length = lax.axis_size(axis)
    return lax.ppermute(x, axis, [(i, (i + by) % length) for i in range(length)])


def line_by_line(dst, src, lines, wide, to, at, start=0):
    for i in range(lines):
        dst[start + i * to : start + i * to + wide, :] = src[i * at : i * at + wide, :]


def columns_beside(x_ref, flat, spread, m, high):
    wide, step = x_ref.shape[0] // high, LINE * m
    flat[...] = x_ref[...].astype(jnp.float32)
    spread[...] = jnp.zeros_like(spread)
    line_by_line(spread, flat, high, wide, step, wide, step)
    rows = spread[...]
    beside = [pltpu.roll(rows, m, 0), rows, pltpu.roll(rows, rows.shape[0] - m, 0)]
    return [part.astype(jnp.bfloat16) for part in beside]


def taps_of(x_ref, flat, spread, m, high):
    step = LINE * m
    rows = high * step
    beside = columns_beside(x_ref, flat, spread, m, high)
    return jnp.concatenate([part[a * step : a * step + rows] for a in range(3) for part in beside], axis=1)


def taps_kernel(blocks, m, high, *refs):
    x_refs, tap_refs, (flat, spread) = refs[:blocks], refs[blocks : 2 * blocks], refs[2 * blocks :]
    for n in range(blocks):
        tap_refs[n][...] = taps_of(x_refs[n], flat, spread, m, high)


def forward_kernel(blocks, m, high, merge, chunk, cast, noted, *refs):
    refs = list(refs)
    x_refs, refs = refs[:blocks], refs[blocks:]
    if noted:
        note_ref, *refs = refs
    if cast:
        w_ref, *refs, kernel_ref, flat, spread = refs
        kernel_ref[...] = w_ref[...].astype(jnp.bfloat16)
        refs = [kernel_ref, *refs, flat, spread]
    wide, step = refs[-2].shape[0] // high, LINE * m
    rows = high * step
    if merge:
        half_ref, peer_ref, *pre_refs, sent_ref, kernel_ref, flat, spread = refs
        count = peer_ref.shape[1]
        half = half_ref[:, chunk * count : (chunk + 1) * count]
        kernel_ref[...] = (0.5 * (half + peer_ref[...].astype(jnp.float32))).astype(jnp.bfloat16)
    else:
        kernel_ref, *pre_refs, sent_ref, flat, spread = refs
    for n in range(blocks):
        lines = x_refs[n][...] if merge else taps_of(x_refs[n], flat, spread, m, high)
        part = jnp.dot(lines, kernel_ref[...], preferred_element_type=jnp.float32)
        for i in range(high):
            pre_refs[n][i * wide : (i + 1) * wide, :] = part[i * step : i * step + wide]
        spot = (n + 1) % blocks if blocks == 2 else n
        if noted:
            sent_ref[spot, : high * wide, :] = pre_refs[n][...].astype(jnp.bfloat16)
        else:
            sent_ref[spot] = pre_refs[n][...].astype(jnp.bfloat16)
    if noted:
        sent_ref[0, high * wide :, :] = note_ref[...]


def beside_each_other(refs):
    return jnp.concatenate([ref[...] for ref in refs], axis=1) if len(refs) > 1 else refs[0][...]


def backward_kernel(blocks, chunks, by_block, notes, now, peers, sends, m, high, classes, scale, step_size, *refs):
    refs = list(refs)

    def take(count):
        return [refs.pop(0) for _ in range(count)]

    x_refs = take(blocks)
    own_refs = [take(blocks) for _ in range(chunks)]
    other_refs = take({True: blocks, False: chunks, None: 0}[by_block])
    note_refs = take(notes)
    label_refs = take(0 if notes else 1)
    head, w_ref, v_ref = take(3)
    peer_refs, sent_refs = take(peers), take(sends)
    half_ref, new_v_ref = take(2)
    grad_refs = take(blocks)
    flat, spread, beside_ref, slope_ref, wide_ref = refs
    wide, step = x_refs[0].shape[0] // high, LINE * m
    rows = high * step
    area = wide // m * high
    depth, chan = w_ref.shape[0] // 3, w_ref.shape[1]
    parts = [pl.ds(a * depth, depth) for a in range(3)]
    turn = lax.broadcasted_iota(jnp.int32, (SUB, chan), 0) % m
    pooled = []
    for n in range(blocks):
        pre = beside_each_other([own_refs[c][n] for c in range(chunks)])
        if by_block is not None:
            other = other_refs[n][0, : flat.shape[0], :] if by_block else jnp.concatenate([ref[n] for ref in other_refs], axis=1)
            pre = pre + other.astype(jnp.float32)
        pre = pre * scale
        sig = jax.nn.sigmoid(pre)
        slope_ref[n] = sig * (1.0 + pre * (1.0 - sig))
        total = jnp.sum((pre * sig).reshape(-1, SUB, chan), axis=0)
        pooled += [jnp.sum(jnp.where(turn == k, total, 0.0), axis=0, keepdims=True) for k in range(m)]
    pooled = (jnp.concatenate(pooled, axis=0) / area).astype(jnp.bfloat16)
    logits = lax.dot_general(pooled, head[...], (((1,), (1,)), ((), ())), preferred_element_type=jnp.float32)
    klass = lax.broadcasted_iota(jnp.int32, logits.shape, 1)
    image = lax.broadcasted_iota(jnp.int32, logits.shape, 0)
    logits = jnp.where(klass < classes, logits, -jnp.inf)
    expo = jnp.exp(logits - jnp.max(logits, axis=1, keepdims=True))
    probs = expo / jnp.sum(expo, axis=1, keepdims=True)
    target = jnp.zeros(logits.shape, jnp.int32)
    for ref in label_refs:
        for n in range(ref.shape[1] * ref.shape[2]):
            target = jnp.where(image == n, ref[now, n // ref.shape[2], n % ref.shape[2]], target)
    if notes:
        for k, note in enumerate([note_refs[0][...], note_refs[1][0, flat.shape[0] :, :]]):
            digits = note.astype(jnp.float32).astype(jnp.int32)
            label = digits[:, : chan // 2] * 32 + digits[:, chan // 2 :]
            label = jnp.concatenate([label] * (head.shape[0] // (chan // 2)), axis=1)
            for n in range(m):
                target = jnp.where(image == k * m + n, label[now * m + n : now * m + n + 1], target)
    onehot = (target == klass).astype(jnp.float32)
    dlogits = (LOSS_SCALE * (probs - onehot)).astype(jnp.bfloat16)
    dpooled = jnp.dot(dlogits, head[...], preferred_element_type=jnp.float32) / area
    right = []
    for n in range(blocks):
        tile = jnp.zeros((SUB, chan), jnp.float32)
        for k in range(m):
            tile = jnp.where(turn == k, dpooled[n * m + k : n * m + k + 1], tile)
        slope_ref[n] = (slope_ref[n].reshape(-1, SUB, chan) * tile[None]).reshape(-1, chan)
        for i in range(high):
            wide_ref[i * step : i * step + wide, :] = slope_ref[n, i * wide : (i + 1) * wide, :]
            wide_ref[i * step + wide : (i + 1) * step, :] = jnp.zeros((step - wide, chan), jnp.float32)
        grad = wide_ref[...].astype(jnp.bfloat16)
        grad_refs[n][...] = grad
        beside = jnp.concatenate(columns_beside(x_refs[n], flat, spread, m, high), axis=1)
        beside_ref[n * (rows + 2 * step) : (n + 1) * (rows + 2 * step), :] = beside
        lines = []
        for a in range(3):
            pieces = [jnp.zeros((a * step, chan), jnp.bfloat16)] if a else []
            pieces.append(grad)
            pieces += [jnp.zeros(((2 - a) * step, chan), jnp.bfloat16)] if a < 2 else []
            lines.append(jnp.concatenate(pieces, axis=0))
        right.append(jnp.concatenate(lines, axis=1))
    total = lax.dot_general(
        beside_ref[...],
        jnp.concatenate(right, axis=0),
        (((0,), (0,)), ((), ())),
        preferred_element_type=jnp.float32,
    )
    for a, p in enumerate(parts):
        move = total[:, a * chan : (a + 1) * chan] * (step_size * scale / LOSS_SCALE)
        new_v = MOMENTUM * v_ref[p, :] - move
        old = w_ref[p, :]
        if peers:
            old = 0.5 * (old + beside_each_other([ref.at[p] for ref in peer_refs]).astype(jnp.float32))
        half = old + MOMENTUM * new_v - move
        for c, ref in enumerate(sent_refs):
            ref[p, :] = half[:, c * (chan // sends) : (c + 1) * (chan // sends)].astype(jnp.bfloat16)
        half_ref[p, :] = half
        new_v_ref[p, :] = new_v


def input_gradient_kernel(blocks, chunks, m, scale, stores, *refs):
    grad_refs, kernel_refs, refs = refs[:blocks], refs[blocks : blocks + chunks], refs[blocks + chunks :]
    if stores:
        v_ref, *out_refs, v_hbm, padded, outs, sem = refs
        store = pltpu.make_async_copy(v_ref, v_hbm, sem)
        store.start()
    else:
        *out_refs, padded, outs = refs
    rows, chan = grad_refs[0].shape
    step = LINE * m
    depth = kernel_refs[0].shape[0] // 3
    share = depth // 3
    edge = jnp.zeros((step, chan), jnp.bfloat16)
    for n in range(blocks):
        padded[n, :step, :] = edge
        padded[n, step : step + rows, :] = grad_refs[n][...]
        padded[n, step + rows :, :] = edge

    def block(n, carry):
        total = None
        for a in range(3):
            term = lax.dot_general(
                padded[n, (2 - a) * step : (2 - a) * step + rows, :],
                beside_each_other([ref.at[a * depth : (a + 1) * depth] for ref in kernel_refs]),
                (((1,), (1,)), ((), ())),
                preferred_element_type=jnp.float32,
            )
            total = term if total is None else total + term
        out = total[:, share : 2 * share]
        out += pltpu.roll(total[:, :share], rows - m, 0)
        out += pltpu.roll(total[:, 2 * share :], m, 0)
        outs[n] = (out * scale).astype(jnp.bfloat16)
        return carry

    lax.fori_loop(0, blocks, block, 0)
    for n in range(blocks):
        out_refs[n][...] = outs[n]
    if stores:
        store.wait()


def split_kernel(turn, share, casts, *refs):
    if casts:
        maps, w_hbm, labels_hbm, mine, theirs, kernel, note, sems, w, w_sems, labels, label_sem = refs
        fetch_labels = pltpu.make_async_copy(labels_hbm, labels, label_sem)
        fetch_labels.start()
        depth = w.shape[0] // w_sems.shape[0]
        parts = [pl.ds(a * depth, depth) for a in range(w_sems.shape[0])]
        fetches = [pltpu.make_async_copy(w_hbm.at[p], w.at[p], w_sems.at[a]) for a, p in enumerate(parts)]
        for copy in fetches:
            copy.start()
    else:
        maps, mine, theirs, sems = refs
    me = lax.axis_index("group")
    copies = []
    for k, (dst, spot) in enumerate([(theirs, 1 - me), (mine, me)]):
        channels = pl.ds(pl.multiple_of(spot * share, share), share)
        copies.append(pltpu.make_async_copy(maps.at[turn, :, :, :, channels], dst, sems.at[k]))
        copies[-1].start()
    if casts:
        for copy, p in zip(fetches, parts):
            copy.wait()
            kernel[p, :] = w[p, :].astype(jnp.bfloat16)
        fetch_labels.wait()
        row, lane = [lax.broadcasted_iota(jnp.int32, note.shape, axis) for axis in range(2)]
        digits = jnp.zeros(note.shape, jnp.int32)
        turns, _, m = labels.shape
        for k in range(turns * m):
            label = labels[k // m, 0, k % m]
            digits = jnp.where(row == k, jnp.where(lane < note.shape[1] // 2, label >> 5, label & 31), digits)
        note[...] = digits.astype(jnp.float32).astype(jnp.bfloat16)
    for copy in copies:
        copy.wait()


def finish_kernel(chunk, blocks, high, wide, share, *refs):
    half_ref, peer_ref, *refs = refs
    refs = refs[1:] if chunk else refs
    block_refs, refs = refs[:blocks], refs[blocks:]
    w_hbm, *refs = refs
    stores = []
    if blocks:
        grads_hbm, w, out_sems, sems = refs
        spots = [lax.axis_index("group"), 1 - lax.axis_index("group")]
        for k, block in enumerate(block_refs):
            channels = pl.ds(pl.multiple_of(spots[k % 2] * share, share), share)
            src = block.at[pl.ds(0, high), pl.ds(0, wide)]
            stores.append(pltpu.make_async_copy(src, grads_hbm.at[k // 2, :, :, :, channels], sems.at[k]))
            stores[-1].start()
    else:
        w, out_sems = refs
    depth, width = w.shape[0] // 3, w.shape[1]
    columns = pl.ds(chunk * width, width)
    for a in range(3):
        p = pl.ds(a * depth, depth)
        w[p, :] = 0.5 * (half_ref[p, columns] + peer_ref[p, :].astype(jnp.float32))
        stores.append(pltpu.make_async_copy(w.at[p], w_hbm.at[p, columns], out_sems.at[a]))
        stores[-1].start()
    for copy in stores:
        copy.wait()


PARAMS = pltpu.CompilerParams(vmem_limit_bytes=24 * 1024 * 1024)
VMEM = pl.BlockSpec(memory_space=pltpu.VMEM)
HBM = pl.BlockSpec(memory_space=pltpu.HBM)
SMEM = pl.BlockSpec(memory_space=pltpu.SMEM)
DMA = pltpu.SemaphoreType.DMA


def f32(*shape, space=jax.ShapeDtypeStruct):
    return space(shape, jnp.float32)


def b16(*shape, space=jax.ShapeDtypeStruct):
    return space(shape, jnp.bfloat16)


def conv_scale(chan):
    return 1.0 / math.sqrt(9 * chan)


def forward(xs, weights, m, high, chunk=0, cast=False, notes=(), wide=0):
    blocks = len(xs)
    depth, chan = weights[-1].shape
    merge = len(weights) == 2
    share = depth // 9
    positions = xs[0].shape[0] // LINE * wide if merge else xs[0].shape[0]
    noted = notes[0].shape[0] if notes else 0
    return pl.pallas_call(
        partial(forward_kernel, blocks, m, high, merge, chunk, cast, len(notes)),
        in_specs=[VMEM] * blocks + [VMEM] * (len(notes) + len(weights)),
        out_shape=[f32(positions, chan)] * blocks
        + [b16(blocks, positions + noted, chan)]
        + [b16(depth, chan)] * (merge or cast),
        scratch_shapes=[
            pltpu.VMEM((positions, share), jnp.float32),
            pltpu.VMEM(((high + 2) * LINE * m, share), jnp.float32),
        ],
        compiler_params=PARAMS,
        cost_estimate=pl.CostEstimate(
            flops=2 * blocks * positions * depth * chan, bytes_accessed=4 * depth * chan, transcendentals=0
        ),
        name="forward",
    )(*xs, *notes, *weights)


def taps_ahead(xs, m, high):
    blocks = len(xs)
    positions, share = xs[0].shape
    space = pltpu.VMEM if blocks == 2 else jax.ShapeDtypeStruct
    return pl.pallas_call(
        partial(taps_kernel, blocks, m, high),
        in_specs=[VMEM] * blocks,
        out_shape=[b16(high * LINE * m, 9 * share, space=space)] * blocks,
        out_specs=[VMEM] * blocks,
        scratch_shapes=[
            pltpu.VMEM((positions, share), jnp.float32),
            pltpu.VMEM(((high + 2) * LINE * m, share), jnp.float32),
        ],
        compiler_params=PARAMS,
        cost_estimate=pl.CostEstimate(flops=1, bytes_accessed=1, transcendentals=0),
        name="taps",
    )(*xs)


def backward(xs, own, other, labels, notes, now, head, w, v, peers, sends, m, high, classes):
    blocks, chunks = len(xs), len(own)
    depth, chan = v.shape
    positions, share = xs[0].shape
    rows = high * LINE * m
    scale = conv_scale(chan)
    step_size = 0.1 * 9 * chan
    by_block = None if len(other) == 0 else other[0].shape[0] == 1
    space = pltpu.VMEM if blocks == 2 else jax.ShapeDtypeStruct
    return pl.pallas_call(
        partial(
            backward_kernel,
            blocks,
            chunks,
            by_block,
            len(notes),
            now,
            len(peers),
            sends,
            m,
            high,
            classes,
            scale,
            step_size,
        ),
        in_specs=[VMEM] * (blocks + blocks * chunks + len(other)) + ([VMEM] * len(notes) or [SMEM]) + [VMEM] * (3 + len(peers)),
        out_shape=[b16(depth, chan // sends)] * sends
        + [f32(depth, chan, space=space)] * 2
        + [b16(rows, chan, space=space)] * blocks,
        out_specs=[VMEM] * (sends + 2 + blocks),
        scratch_shapes=[
            pltpu.VMEM((positions, share), jnp.float32),
            pltpu.VMEM((rows + 2 * LINE * m, share), jnp.float32),
            pltpu.VMEM((blocks * (rows + 2 * LINE * m), 3 * share), jnp.bfloat16),
            pltpu.VMEM((blocks, positions, chan), jnp.float32),
            pltpu.VMEM((rows, chan), jnp.float32),
        ],
        compiler_params=PARAMS,
        cost_estimate=pl.CostEstimate(
            flops=2 * blocks * rows * v.size, bytes_accessed=20 * v.size, transcendentals=blocks * rows * chan
        ),
        name="backward",
    )(*xs, *sum(own, []), *other, *(notes or [labels]), head, w, v, *peers)


def input_gradient(grads, kernel, m, v=()):
    blocks = len(grads)
    rows, chan = grads[0].shape
    share = kernel[0].shape[0] // 9
    stores = len(v)
    return pl.pallas_call(
        partial(input_gradient_kernel, blocks, len(kernel), m, conv_scale(chan), stores),
        in_specs=[VMEM] * (blocks + len(kernel)) + [pl.BlockSpec(memory_space=pl.ANY)] * stores,
        out_shape=[b16(rows, share)] * blocks + [f32(*x.shape, space=pltpu.HBM) for x in v],
        out_specs=[VMEM] * blocks + [HBM] * stores,
        scratch_shapes=[
            pltpu.VMEM((blocks, rows + 2 * LINE * m, chan), jnp.bfloat16),
            pltpu.VMEM((blocks, rows, share), jnp.bfloat16),
        ]
        + [DMA] * stores,
        compiler_params=PARAMS,
        cost_estimate=pl.CostEstimate(flops=1, bytes_accessed=1, transcendentals=0),
        name="input_gradient",
    )(*grads, *kernel, *v)


def split(maps, turn, w=None, labels=None):
    _, high, wide, m, chan = maps.shape
    share = chan // 2
    arrays, outs, scratch = [maps], [b16(high, wide, m, share)] * 2, [DMA((2,))]
    casts = w is not None
    if casts:
        arrays += [w, labels]
        rows = labels.size + -(high * wide * m + labels.size) % 16
        outs += [b16(*w.shape, space=pltpu.VMEM), b16(rows, chan, space=pltpu.VMEM)]
        scratch += [pltpu.VMEM(w.shape, jnp.float32), DMA((6,)), pltpu.SMEM(labels.shape, jnp.int32), DMA]
    mine, theirs, *more = pl.pallas_call(
        partial(split_kernel, turn, share, casts),
        in_specs=[pl.BlockSpec(memory_space=pl.ANY)] * len(arrays),
        out_shape=outs,
        out_specs=[pl.BlockSpec(memory_space=pl.ANY)] * 2 + [VMEM] * len(outs[2:]),
        scratch_shapes=scratch,
        compiler_params=PARAMS,
        cost_estimate=pl.CostEstimate(flops=1, bytes_accessed=1, transcendentals=0),
        name="split",
    )(*arrays)
    return mine.reshape(-1, share), theirs.reshape(-1, share), *more


def finish(half, peers, blocks, high, wide, m):
    depth, chan = half.shape
    share = depth // 9
    blocks = [block.reshape(high, LINE, m, share) for block in blocks]
    w, grads = [], []
    for c, peer in enumerate(peers):
        here = blocks if c == 0 else []
        outs = [f32(depth, chan, space=pltpu.HBM)]
        outs += [b16(ITERS, high, wide, m, chan, space=pltpu.HBM)] if here else []
        *w, = pl.pallas_call(
            partial(finish_kernel, c, len(here), high, wide, share),
            in_specs=[VMEM] * 2 + [pl.BlockSpec(memory_space=pl.ANY)] * (len(w) + len(here)),
            out_shape=outs,
            out_specs=[HBM] * len(outs),
            scratch_shapes=[pltpu.VMEM((depth, chan // CHUNKS), jnp.float32), DMA((3,))]
            + [DMA((2 * ITERS,))] * (len(here) > 0),
            input_output_aliases={2: 0} if w else {},
            compiler_params=PARAMS,
            cost_estimate=pl.CostEstimate(flops=1, bytes_accessed=1, transcendentals=0),
            name="finish",
        )(half, peer, *w, *here)
        grads, w = grads or w[1:], w[:1]
    return w[0], grads[0] if grads else None


def run(position, images, labels, weights, velocity, head_weight):
    shape = weights.shape
    maps = jnp.transpose(images[:, 0], (0, 2, 3, 1, 4))
    _, high, wide, m, chan = maps.shape
    share = shape[3]
    members = lax.axis_size("group")
    bits = lax.axis_size("replica").bit_length() - 1
    classes = head_weight.shape[0]
    pair = members == 2
    w = weights.reshape(9 * share, chan)
    v = velocity.reshape(9 * share, chan)
    head = jnp.pad(head_weight, ((0, -classes % 128), (0, 0)))

    def flat(part):
        return part.reshape(high * wide * m, share)

    def send_back(parts):
        parts = [part.reshape(high, LINE, m, share)[:, :wide] for part in parts]
        parts = lax.all_to_all(jnp.stack(parts), "group", split_axis=0, concat_axis=0, tiled=True)
        return jnp.concatenate([parts[k] for k in range(members)], axis=3)

    if pair:
        mine, theirs, kernel, note = split(maps, 0, w, labels)
        came = shifted(theirs, "group", 1)
        xs = [mine, came]
    else:
        shares = maps.reshape(ITERS, high, wide, m, members, share)
        shares = lax.all_to_all(shares, "group", split_axis=4, concat_axis=4, tiled=True)
        labels = lax.all_gather(labels, "group", axis=1, tiled=True)
        xs, later = [[flat(shares[t, :, :, :, k]) for k in range(members)] for t in range(ITERS)]

    def add_up(own, sent):
        if pair:
            return own, [shifted(sent, "group", 1)]
        return [lax.psum(part, "group") for part in own], []

    notes = []
    if pair:
        own_a, sent_a = forward([mine], [kernel], m, high, notes=[note])
        other_b = shifted(sent_a, "group", 1)
        own_b, sent_b = forward([came], [kernel], m, high)
        other_a = shifted(sent_b, "group", 1)
        own, other, notes = [own_a, own_b], [other_a, other_b], [note, other_b]
    else:
        *own, sent, kernel = forward(xs, [w], m, high, cast=True)
        own, other = add_up(own, sent)
    made = backward(xs, [own], other, labels, notes, 0, head, w, v, [], CHUNKS, m, high, classes)
    sent, (half, v), grads = made[:CHUNKS], made[CHUNKS : CHUNKS + 2], made[CHUNKS + 2 :]
    old_kernel = [kernel]
    peers = [shifted(part, "replica", 1 << position) for part in sent]
    if pair:
        mine, theirs = split(maps, 1)
        xs = [mine, shifted(theirs, "group", 1)]
    else:
        xs = later
    taps = taps_ahead(xs, m, high)
    own, other, kernel = [], [], []
    for chunk, peer in enumerate(peers):
        *parts, sent, part = forward(taps, [half, peer], m, high, chunk, wide=wide)
        parts, came = add_up(parts, sent)
        own.append(parts)
        other += came
        kernel.append(part)
    grads, sent = lax.optimization_barrier((grads, sent))
    parts = input_gradient(grads, old_kernel, m)
    made = backward(xs, own, other, labels, notes, 1, head, half, v, peers, CHUNKS, m, high, classes)
    sent, (half, v), grads = made[:CHUNKS], made[CHUNKS : CHUNKS + 2], made[CHUNKS + 2 :]
    if pair:
        parts, sent = lax.optimization_barrier((parts, sent))
    peers = [shifted(part, "replica", 1 << (position + 1) % bits) for part in sent]
    *last, v = input_gradient(grads, kernel, m, [v])
    if pair:
        blocks = [parts[0], shifted(parts[1], "group", 1), last[0], shifted(last[1], "group", 1)]
        w, grads_in = finish(half, peers, blocks, high, wide, m)
    else:
        w, _ = finish(half, peers, [], high, wide, m)
        grads_in = jnp.stack([send_back(parts), send_back(last)])
    grads_in = jnp.transpose(grads_in, (0, 3, 1, 2, 4))[:, None]
    return (w.reshape(shape), v.reshape(shape), grads_in)


def local(images, labels, step_index, weights, velocity, head_weight):
    bits = lax.axis_size("replica").bit_length() - 1
    branches = [partial(run, position) for position in range(bits)]
    return lax.switch(step_index[0] % bits, branches, images, labels, weights, velocity, head_weight)


def solution(mesh):
    return jax.shard_map(
        local,
        mesh=mesh,
        in_specs=(
            P(None, "replica", "group", None, None, None),
            P(None, "replica", "group"),
            P(),
            P("replica", None, None, "group", None),
            P("replica", None, None, "group", None),
            P(),
        ),
        out_specs=(
            P("replica", None, None, "group", None),
            P("replica", None, None, "group", None),
            P(None, "replica", "group", None, None, None),
        ),
        check_vma=False,
    )
```
